32 devices in a mesh: pop: 8 (over z, y), col: 4 (over x, core).
Axes of the slice: x: 2, y: 2, z: 4, core: 2. Of those that a mesh axis runs over, the one named last changes fastest.
Arguments:
- weight: float32 [2304, 16384], P('pop', 'col'), may hold values from -3 to 3
- row_factors: bfloat16 [2304, 768], P(None, 'pop'), may hold values from -6 to 6
- col_factors: bfloat16 [768, 16384], P('pop', 'col'), may hold values from -6 to 6
- fitness_ranks: int32 [768], P('pop'), may hold values from 0 to 767, each once
Outputs:
- new_weight: float32 [2304, 16384], P('pop', 'col')
The draws below stay inside these ranges and needn't reach their ends.
Inputs may be any that keep to these rules, and one draw needn't show every extreme that they name: fitness_ranks holds each of 0 to 767 exactly once.
All inputs are finite; a program needn't handle non-finite values.
Results may differ from the reference program's by a relative error of at most 0.0026.
Values may be sent and summed in bfloat16 or wider, within the bound.
A program may use at most 64 MiB of HBM per device.

```python
import math
import jax
import jax.numpy as jnp

D = 2304
F = 16384
MEMB = 768


def with_spikes(entries, stream_key, source, target, shards_of, factor):
    owner, partner = [(jnp.arange(entries.shape[position]) // (entries.shape[position] // shards_of)).reshape([-1 if axis == position else 1 for axis in range(entries.ndim)]) for position in (source, target)]
    chosen = jax.random.permutation(stream_key, shards_of)[partner]
    strong = (owner == chosen) | (owner == (partner + shards_of // 2) % shards_of)
    return jnp.where(strong, factor * entries, entries)


def block_levels(key, dims, split, least, top_value):
    def one(position, parts):
        steps = jax.random.uniform(jax.random.fold_in(jax.random.fold_in(key, 6), position), (parts,), jnp.float32, least / len(split), top_value / len(split))
        return jnp.repeat(jnp.exp(steps), dims[position] // parts).reshape((-1,) + (1,) * (len(dims) - position - 1))

    gain = one(*split[0])
    for cut in split[1:]:
        gain = gain * one(*cut)
    return gain


def centred(own_key, extent, deviation, reach, shards=(), held_as=jnp.bfloat16):
    result = deviation * jax.random.normal(own_key, extent, jnp.float32)
    if shards:
        result = result * block_levels(own_key, extent, shards, -0.22, 0.18)
    return jnp.clip(result, -reach, reach).astype(held_as)


def bell_draw_with(key, shape, deviation, bound, cuts, heavy, kind=jnp.bfloat16):
    drawn = deviation * jax.random.normal(key, shape, jnp.float32)
    if cuts:
        drawn = drawn * block_levels(key, shape, cuts, -0.22, 0.18)
    return jnp.clip(with_spikes(drawn, jax.random.fold_in(key, 3), *heavy), -bound, bound).astype(kind)


def setup_inputs(seed: int = 0) -> dict:
    seeds = jax.random.split(jax.random.key(seed), 5)
    return {
        "weight": centred(seeds[0], (D, F), 0.5, 3.0, ((0, 8), (1, 4)), jnp.float32),
        "row_factors": bell_draw_with(seeds[1], (D, MEMB), 1.0, 6.0, ((1, 8),), (1, 0, 8, 2.0)),
        "col_factors": centred(seeds[2], (MEMB, F), 1.0, 6.0, ((0, 8), (1, 4))),
        "fitness_ranks": jax.random.permutation(seeds[3], MEMB).astype(jnp.int32),
    }


def reference(weight, row_factors, col_factors, fitness_ranks):
    shaped = fitness_ranks.astype(jnp.float32) / (MEMB - 1) - 0.5
    scaled = (shaped[:, None] * col_factors.astype(jnp.float32)).astype(jnp.bfloat16)
    update = jnp.dot(row_factors, scaled, preferred_element_type=jnp.float32)
    return weight + 3.0 / math.sqrt(MEMB) * update
```

```python
import functools
import math

import jax
import jax.numpy as jnp
from jax import lax
from jax.experimental import pallas as pl
from jax.experimental.pallas import tpu as pltpu
from jax.sharding import PartitionSpec as P

MESH = pl.DeviceIdType.MESH
WIDTH = 256
LAG = 2


def kernel(zc, members, ranks_ref, rf_ref, col_ref, w_ref, out_ref,
           shaped, colv, g, rfl, ysend, yrecv, own, wv,
           sem_in, sem_out, left_send, left_recv, right_send, right_recv,
           rf_send, rf_recv, fwd_send, fwd_recv, y_send, y_recv):
    mb, cols = colv.shape
    kb = rf_ref.shape[1]
    rows = own.shape[0]
    nch = cols // WIDTH
    scale = 3.0 / math.sqrt(members)
    me = lax.axis_index("pop")
    c = lax.axis_index("col")
    z, y = me // 2, me % 2
    half = c % 2
    mate = c + 1 - 2 * half
    partner = me + 1 - 2 * y

    col_in = pltpu.make_async_copy(col_ref, colv, sem_in.at[0])
    w_in = pltpu.make_async_copy(w_ref, wv, sem_in.at[1])
    col_in.start()
    w_in.start()

    barrier = pltpu.get_barrier_semaphore()
    for dz in range(1, zc):
        other = lax.rem(z + dz, zc) * 2 + y
        pl.semaphore_signal(barrier, inc=1, device_id=(other, c), device_id_type=MESH)
    pl.semaphore_signal(barrier, inc=1, device_id=(partner, c), device_id_type=MESH)
    pl.semaphore_signal(barrier, inc=1, device_id=(me, mate), device_id_type=MESH)

    flat = jnp.broadcast_to(ranks_ref[...].astype(jnp.float32), (mb, mb))
    eye = lax.broadcasted_iota(jnp.int32, (mb, mb), 0) == lax.broadcasted_iota(jnp.int32, (mb, mb), 1)
    rank = jnp.sum(jnp.where(eye, flat, 0.0), axis=1, keepdims=True)
    shaped[...] = jnp.broadcast_to(rank / (members - 1) - 0.5, shaped.shape)
    col_in.wait()
    pl.semaphore_wait(barrier, zc + 1)

    def chunk(j):
        return pl.ds(pl.multiple_of(j * WIDTH, WIDTH), WIDTH)

    def block_copy(b, j, send, recv, target):
        piece = g.at[b, pl.ds(0, mb), chunk(j)]
        return pltpu.make_async_remote_copy(
            src_ref=piece, dst_ref=piece, send_sem=send, recv_sem=recv,
            device_id=(target * 2 + y, c), device_id_type=MESH)

    def left_copy(d, j):
        return block_copy(z + d, j, left_send.at[d, j], left_recv.at[d + 1, j], z - 1)

    def right_copy(d, j):
        return block_copy(z - d, j, right_send.at[d, j], right_recv.at[d + 1, j], z + 1)

    def arrival(b, j, recv):
        piece = g.at[b, pl.ds(0, mb), chunk(j)]
        return pltpu.make_async_copy(piece, piece, recv)

    def rf_copy(dz):
        to = lax.rem(z + dz, zc)
        src = rf_ref.at[pl.ds(pl.multiple_of((to * 2 + half) * rows, 16), rows)]
        dst = rfl.at[z, pl.ds(pl.multiple_of(half * rows, 16), rows)]
        return pltpu.make_async_remote_copy(
            src_ref=src, dst_ref=dst, send_sem=rf_send.at[dz], recv_sem=rf_recv.at[dz],
            device_id=(to * 2 + y, c), device_id_type=MESH)

    def fwd_copy(dz):
        origin = lax.rem(z + zc - dz, zc)
        piece = rfl.at[origin, pl.ds(pl.multiple_of(half * rows, 16), rows)]
        return pltpu.make_async_remote_copy(
            src_ref=piece, dst_ref=piece, send_sem=fwd_send.at[dz], recv_sem=fwd_recv.at[dz],
            device_id=(me, mate), device_id_type=MESH)

    def fwd_arrival(dz):
        origin = lax.rem(z + zc - dz, zc)
        piece = rfl.at[origin, pl.ds(pl.multiple_of((1 - half) * rows, 16), rows)]
        return pltpu.make_async_copy(piece, piece, fwd_recv.at[dz])

    def y_copy(j):
        return pltpu.make_async_remote_copy(
            src_ref=ysend.at[:, chunk(j)], dst_ref=yrecv.at[:, chunk(j)],
            send_sem=y_send.at[j], recv_sem=y_recv.at[j],
            device_id=(partner, c), device_id_type=MESH)

    def out_copy(j):
        return pltpu.make_async_copy(own.at[:, chunk(j)], out_ref.at[:, chunk(j)], sem_out.at[j])

    for dz in range(1, zc):
        rf_copy(dz).start()

    def lhs(which):
        at = pl.ds(pl.multiple_of(which * rows, 16), rows)
        return jnp.concatenate([rfl[o, at, :] for o in range(zc)], axis=1)

    def tick(t, carry):
        @pl.when(t < nch)
        def _():
            at = chunk(t)
            g[z, pl.ds(0, mb), at] = (shaped[:, 0:1] * colv[:, at].astype(jnp.float32)).astype(jnp.bfloat16)

            @pl.when(z > 0)
            def _():
                left_copy(0, t).start()

            @pl.when(z < zc - 1)
            def _():
                right_copy(0, t).start()

        @pl.when(t == 0)
        def _():
            if kb > mb:
                g[:, pl.ds(mb, kb - mb), :] = jnp.zeros((zc, kb - mb, cols), jnp.bfloat16)
            rfl[z] = rf_ref[pl.ds(pl.multiple_of(z * 2 * rows, 16), 2 * rows), :]

        @pl.when(t == 1)
        def _():
            for dz in range(1, zc):
                rf_copy(dz).wait_recv()
                fwd_copy(dz).start()

        for d in range(1, zc):
            j = t - d

            @pl.when((j >= 0) & (j < nch))
            def _():
                @pl.when(z + d < zc)
                def _():
                    arrival(z + d, j, left_recv.at[d, j]).wait()
                    if d < zc - 1:
                        @pl.when(z > 0)
                        def _():
                            left_copy(d, j).start()

                @pl.when(z - d >= 0)
                def _():
                    arrival(z - d, j, right_recv.at[d, j]).wait()
                    if d < zc - 1:
                        @pl.when(z < zc - 1)
                        def _():
                            right_copy(d, j).start()

        jc = t - (zc - 1)

        @pl.when(jc == 0)
        def _():
            for dz in range(1, zc):
                fwd_arrival(dz).wait()

        @pl.when((jc >= 0) & (jc < nch))
        def _():
            at = chunk(jc)
            rhs = g[:, :, at].reshape(zc * kb, WIDTH)
            ysend[:, at] = jnp.dot(lhs(1 - y), rhs, preferred_element_type=jnp.float32).astype(jnp.bfloat16)
            y_copy(jc).start()
            own[:, at] = jnp.dot(lhs(y), rhs, preferred_element_type=jnp.float32)

        jf = jc - LAG

        @pl.when(jf == 0)
        def _():
            w_in.wait()

        @pl.when(jf >= 0)
        def _():
            at = chunk(jf)
            y_copy(jf).wait_recv()
            own[:, at] = wv[:, at] + scale * (own[:, at] + yrecv[:, at].astype(jnp.float32))
            out_copy(jf).start()

        return carry

    lax.fori_loop(0, nch + zc - 1 + LAG, tick, 0)

    def drain(j, carry):
        for d in range(zc - 1):
            @pl.when((z + d < zc) & (z > 0))
            def _():
                left_copy(d, j).wait_send()

            @pl.when((z - d >= 0) & (z < zc - 1))
            def _():
                right_copy(d, j).wait_send()
        y_copy(j).wait_send()
        out_copy(j).wait()
        return carry

    lax.fori_loop(0, nch, drain, 0)
    for dz in range(1, zc):
        rf_copy(dz).wait_send()
        fwd_copy(dz).wait_send()


def body(weight, row_factors, col_factors, fitness_ranks):
    pop = lax.axis_size("pop")
    mb = fitness_ranks.shape[0]
    members = mb * pop
    zc = pop // 2
    rows, cols = weight.shape
    kb = -(-mb // 128) * 128
    nch = cols // WIDTH
    padded = jnp.pad(row_factors, ((0, 0), (0, kb - mb)))
    anywhere = pl.BlockSpec(memory_space=pl.ANY)
    vmem = pl.BlockSpec(memory_space=pltpu.VMEM)
    dma = pltpu.SemaphoreType.DMA
    return pl.pallas_call(
        functools.partial(kernel, zc, members),
        out_shape=jax.ShapeDtypeStruct((rows, cols), jnp.float32),
        in_specs=[vmem, vmem, anywhere, anywhere],
        out_specs=anywhere,
        scratch_shapes=[
            pltpu.VMEM((mb, 128), jnp.float32),
            pltpu.VMEM((mb, cols), jnp.bfloat16),
            pltpu.VMEM((zc, kb, cols), jnp.bfloat16),
            pltpu.VMEM((zc, 2 * rows, kb), jnp.bfloat16),
            pltpu.VMEM((rows, cols), jnp.bfloat16),
            pltpu.VMEM((rows, cols), jnp.bfloat16),
            pltpu.VMEM((rows, cols), jnp.float32),
            pltpu.VMEM((rows, cols), jnp.float32),
            dma((2,)), dma((nch,)),
            dma((zc, nch)), dma((zc, nch)), dma((zc, nch)), dma((zc, nch)),
            dma((zc,)), dma((zc,)), dma((zc,)), dma((zc,)),
            dma((nch,)), dma((nch,)),
        ],
        compiler_params=pltpu.CompilerParams(
            collective_id=0, has_side_effects=True, vmem_limit_bytes=56 * 1024 * 1024),
        cost_estimate=pl.CostEstimate(
            flops=2 * rows * cols * members, bytes_accessed=8 * rows * cols, transcendentals=0),
    )(fitness_ranks.reshape(1, mb), padded, col_factors, weight)


def solution(mesh):
    in_specs = (P("pop", "col"), P(None, "pop"), P("pop", "col"), P("pop"))
    out_specs = P("pop", "col")
    return jax.shard_map(body, mesh=mesh, in_specs=in_specs, out_specs=out_specs, check_vma=False)
```

```python
import functools
import math

import jax
import jax.numpy as jnp
from jax import lax
from jax.experimental import pallas as pl
from jax.experimental.pallas import tpu as pltpu
from jax.sharding import PartitionSpec as P

MESH = pl.DeviceIdType.MESH
WIDTH = 256
LAG = 2


def kernel(zc, members, ranks_ref, rft_ref, col_ref, w_ref, own,
           shaped, rf_ref, colv, g, rfl, ysend, yrecv, wv, sem_in, left_send, left_recv, right_send, right_recv,
           rf_send, rf_recv, fwd_send, fwd_recv, y_send, y_recv):
    mb, cols = colv.shape
    kb = rf_ref.shape[1]
    rows = own.shape[0]
    nch = cols // WIDTH
    scale = 3.0 / math.sqrt(members)
    me = lax.axis_index("pop")
    c = lax.axis_index("col")
    z, y = me // 2, me % 2
    half = c % 2
    mate = c + 1 - 2 * half
    partner = me + 1 - 2 * y

    col_in = pltpu.make_async_copy(col_ref, colv, sem_in.at[0])
    w_in = pltpu.make_async_copy(w_ref, wv, sem_in.at[1])
    col_in.start()

    barrier = pltpu.get_barrier_semaphore()
    for dz in range(1, zc):
        other = lax.rem(z + dz, zc) * 2 + y
        pl.semaphore_signal(barrier, inc=1, device_id=(other, c), device_id_type=MESH)
    pl.semaphore_signal(barrier, inc=1, device_id=(partner, c), device_id_type=MESH)
    pl.semaphore_signal(barrier, inc=1, device_id=(me, mate), device_id_type=MESH)

    flat = jnp.broadcast_to(ranks_ref[...].astype(jnp.float32), (mb, mb))
    eye = lax.broadcasted_iota(jnp.int32, (mb, mb), 0) == lax.broadcasted_iota(jnp.int32, (mb, mb), 1)
    rank = jnp.sum(jnp.where(eye, flat, 0.0), axis=1, keepdims=True)
    shaped[...] = jnp.broadcast_to(rank / (members - 1) - 0.5, shaped.shape)
    for at in range(0, rf_ref.shape[0], 128):
        part = rft_ref[:, at:at + 128].astype(jnp.float32)
        if kb > mb:
            part = jnp.concatenate([part, jnp.zeros((kb - mb, 128), jnp.float32)], axis=0)
        rf_ref[at:at + 128, :] = part.T.astype(jnp.bfloat16)
    col_in.wait()
    pl.semaphore_wait(barrier, zc + 1)

    def chunk(j):
        return pl.ds(pl.multiple_of(j * WIDTH, WIDTH), WIDTH)

    def block_copy(b, j, send, recv, target):
        piece = g.at[b, pl.ds(0, mb), chunk(j)]
        return pltpu.make_async_remote_copy(
            src_ref=piece, dst_ref=piece, send_sem=send, recv_sem=recv,
            device_id=(target * 2 + y, c), device_id_type=MESH)

    def left_copy(d, j):
        return block_copy(z + d, j, left_send.at[d, j], left_recv.at[d + 1, j], z - 1)

    def right_copy(d, j):
        return block_copy(z - d, j, right_send.at[d, j], right_recv.at[d + 1, j], z + 1)

    def arrival(b, j, recv):
        piece = g.at[b, pl.ds(0, mb), chunk(j)]
        return pltpu.make_async_copy(piece, piece, recv)

    def rf_copy(dz):
        to = lax.rem(z + dz, zc)
        src = rf_ref.at[pl.ds(pl.multiple_of((to * 2 + half) * rows, 16), rows)]
        dst = rfl.at[z, pl.ds(pl.multiple_of(half * rows, 16), rows)]
        return pltpu.make_async_remote_copy(
            src_ref=src, dst_ref=dst, send_sem=rf_send.at[dz], recv_sem=rf_recv.at[dz],
            device_id=(to * 2 + y, c), device_id_type=MESH)

    def fwd_copy(dz):
        origin = lax.rem(z + zc - dz, zc)
        piece = rfl.at[origin, pl.ds(pl.multiple_of(half * rows, 16), rows)]
        return pltpu.make_async_remote_copy(
            src_ref=piece, dst_ref=piece, send_sem=fwd_send.at[dz], recv_sem=fwd_recv.at[dz],
            device_id=(me, mate), device_id_type=MESH)

    def fwd_arrival(dz):
        origin = lax.rem(z + zc - dz, zc)
        piece = rfl.at[origin, pl.ds(pl.multiple_of((1 - half) * rows, 16), rows)]
        return pltpu.make_async_copy(piece, piece, fwd_recv.at[dz])

    def y_copy(j):
        return pltpu.make_async_remote_copy(
            src_ref=ysend.at[:, chunk(j)], dst_ref=yrecv.at[:, chunk(j)],
            send_sem=y_send.at[j], recv_sem=y_recv.at[j],
            device_id=(partner, c), device_id_type=MESH)

    for dz in range(1, zc):
        rf_copy(dz).start()
    w_in.start()

    def lhs(which):
        at = pl.ds(pl.multiple_of(which * rows, 16), rows)
        return jnp.concatenate([rfl[o, at, :] for o in range(zc)], axis=1)

    def tick(t, carry):
        @pl.when(t < nch)
        def _():
            at = chunk(t)
            g[z, pl.ds(0, mb), at] = (shaped[:, 0:1] * colv[:, at].astype(jnp.float32)).astype(jnp.bfloat16)

            @pl.when(z > 0)
            def _():
                left_copy(0, t).start()

            @pl.when(z < zc - 1)
            def _():
                right_copy(0, t).start()

        @pl.when(t == 0)
        def _():
            if kb > mb:
                g[:, pl.ds(mb, kb - mb), :] = jnp.zeros((zc, kb - mb, cols), jnp.bfloat16)
            rfl[z] = rf_ref[pl.ds(pl.multiple_of(z * 2 * rows, 16), 2 * rows), :]

        for d in range(1, zc):
            j = t - d

            @pl.when((j >= 0) & (j < nch))
            def _():
                @pl.when(z + d < zc)
                def _():
                    arrival(z + d, j, left_recv.at[d, j]).wait()
                    if d < zc - 1:
                        @pl.when(z > 0)
                        def _():
                            left_copy(d, j).start()

                @pl.when(z - d >= 0)
                def _():
                    arrival(z - d, j, right_recv.at[d, j]).wait()
                    if d < zc - 1:
                        @pl.when(z < zc - 1)
                        def _():
                            right_copy(d, j).start()

        @pl.when(t == 1)
        def _():
            for dz in range(1, zc):
                rf_copy(dz).wait_recv()
                fwd_copy(dz).start()

        jc = t - (zc - 1)

        @pl.when(jc == 0)
        def _():
            for dz in range(1, zc):
                fwd_arrival(dz).wait()

        @pl.when((jc >= 0) & (jc < nch))
        def _():
            at = chunk(jc)
            rhs = g[:, :, at].reshape(zc * kb, WIDTH)
            ysend[:, at] = jnp.dot(lhs(1 - y), rhs, preferred_element_type=jnp.float32).astype(jnp.bfloat16)
            y_copy(jc).start()
            own[:, at] = jnp.dot(lhs(y), rhs, preferred_element_type=jnp.float32)

        jf = jc - LAG

        @pl.when(jf == 0)
        def _():
            w_in.wait()

        @pl.when(jf >= 0)
        def _():
            at = chunk(jf)
            y_copy(jf).wait_recv()
            own[:, at] = wv[:, at] + scale * (own[:, at] + yrecv[:, at].astype(jnp.float32))

        return carry

    lax.fori_loop(0, nch + zc - 1 + LAG, tick, 0)

    def drain(j, carry):
        for d in range(zc - 1):
            @pl.when((z + d < zc) & (z > 0))
            def _():
                left_copy(d, j).wait_send()

            @pl.when((z - d >= 0) & (z < zc - 1))
            def _():
                right_copy(d, j).wait_send()
        y_copy(j).wait_send()
        return carry

    lax.fori_loop(0, nch, drain, 0)
    for dz in range(1, zc):
        rf_copy(dz).wait_send()
        fwd_copy(dz).wait_send()


def body(weight, row_factors, col_factors, fitness_ranks):
    pop = lax.axis_size("pop")
    mb = fitness_ranks.shape[0]
    members = mb * pop
    zc = pop // 2
    rows, cols = weight.shape
    kb = -(-mb // 128) * 128
    nch = cols // WIDTH
    anywhere = pl.BlockSpec(memory_space=pl.ANY)
    vmem = pl.BlockSpec(memory_space=pltpu.VMEM)
    dma = pltpu.SemaphoreType.DMA
    return pl.pallas_call(
        functools.partial(kernel, zc, members),
        out_shape=pltpu.VMEM((rows, cols), jnp.float32),
        in_specs=[vmem, vmem, anywhere, anywhere],
        out_specs=vmem,
        scratch_shapes=[
            pltpu.VMEM((mb, 128), jnp.float32),
            pltpu.VMEM((row_factors.shape[0], kb), jnp.bfloat16),
            pltpu.VMEM((mb, cols), jnp.bfloat16),
            pltpu.VMEM((zc, kb, cols), jnp.bfloat16),
            pltpu.VMEM((zc, 2 * rows, kb), jnp.bfloat16),
            pltpu.VMEM((rows, cols), jnp.bfloat16),
            pltpu.VMEM((rows, cols), jnp.bfloat16),
            pltpu.VMEM((rows, cols), jnp.float32),
            dma((2,)),
            dma((zc, nch)), dma((zc, nch)), dma((zc, nch)), dma((zc, nch)),
            dma((zc,)), dma((zc,)), dma((zc,)), dma((zc,)),
            dma((nch,)), dma((nch,)),
        ],
        compiler_params=pltpu.CompilerParams(
            collective_id=0, has_side_effects=True, vmem_limit_bytes=56 * 1024 * 1024),
        cost_estimate=pl.CostEstimate(
            flops=2 * rows * cols * members, bytes_accessed=8 * rows * cols, transcendentals=0),
    )(fitness_ranks.reshape(1, mb), row_factors.T, col_factors, weight)


def solution(mesh):
    in_specs = (P("pop", "col"), P(None, "pop"), P("pop", "col"), P("pop"))
    out_specs = P("pop", "col")
    return jax.shard_map(body, mesh=mesh, in_specs=in_specs, out_specs=out_specs, check_vma=False)
```

```python
import functools
import math

import jax
import jax.numpy as jnp
from jax import lax
from jax.experimental import pallas as pl
from jax.experimental.pallas import tpu as pltpu
from jax.sharding import PartitionSpec as P

MESH = pl.DeviceIdType.MESH
WIDTH = 256
LAG = 2


def kernel(zc, members, ranks_ref, rft_ref, col_ref, w_ref, own,
           shaped, rf_ref, colv, g, rfl, ysend, yrecv, wv, sem_in, left_send, left_recv, right_send, right_recv,
           rf_send, rf_recv, fwd_send, fwd_recv, y_send, y_recv):
    mb, cols = colv.shape
    kb = rf_ref.shape[1]
    rows = own.shape[0]
    nch = cols // WIDTH
    scale = 3.0 / math.sqrt(members)
    me = lax.axis_index("pop")
    c = lax.axis_index("col")
    z, y = me // 2, me % 2
    half = c % 2
    mate = c + 1 - 2 * half
    partner = me + 1 - 2 * y

    col_in = pltpu.make_async_copy(col_ref, colv, sem_in.at[0])
    w_in = pltpu.make_async_copy(w_ref, wv, sem_in.at[1])
    col_in.start()

    barrier = pltpu.get_barrier_semaphore()
    for dz in range(1, zc):
        other = lax.rem(z + dz, zc) * 2 + y
        pl.semaphore_signal(barrier, inc=1, device_id=(other, c), device_id_type=MESH)
    pl.semaphore_signal(barrier, inc=1, device_id=(partner, c), device_id_type=MESH)
    pl.semaphore_signal(barrier, inc=1, device_id=(me, mate), device_id_type=MESH)

    flat = jnp.broadcast_to(ranks_ref[...].astype(jnp.float32), (mb, mb))
    eye = lax.broadcasted_iota(jnp.int32, (mb, mb), 0) == lax.broadcasted_iota(jnp.int32, (mb, mb), 1)
    rank = jnp.sum(jnp.where(eye, flat, 0.0), axis=1, keepdims=True)
    shaped[...] = jnp.broadcast_to(rank / (members - 1) - 0.5, shaped.shape)
    for at in range(0, rf_ref.shape[0], 128):
        part = rft_ref[:, at:at + 128].astype(jnp.float32)
        if kb > mb:
            part = jnp.concatenate([part, jnp.zeros((kb - mb, 128), jnp.float32)], axis=0)
        rf_ref[at:at + 128, :] = part.T.astype(jnp.bfloat16)
    col_in.wait()
    pl.semaphore_wait(barrier, zc + 1)

    def chunk(j):
        return pl.ds(pl.multiple_of(j * WIDTH, WIDTH), WIDTH)

    def block_copy(b, j, send, recv, target):
        piece = g.at[j, b, pl.ds(0, mb), :]
        return pltpu.make_async_remote_copy(
            src_ref=piece, dst_ref=piece, send_sem=send, recv_sem=recv,
            device_id=(target * 2 + y, c), device_id_type=MESH)

    def left_copy(d, j):
        return block_copy(z + d, j, left_send.at[d, j], left_recv.at[d + 1, j], z - 1)

    def right_copy(d, j):
        return block_copy(z - d, j, right_send.at[d, j], right_recv.at[d + 1, j], z + 1)

    def arrival(b, j, recv):
        piece = g.at[j, b, pl.ds(0, mb), :]
        return pltpu.make_async_copy(piece, piece, recv)

    def rf_copy(dz):
        to = lax.rem(z + dz, zc)
        src = rf_ref.at[pl.ds(pl.multiple_of((to * 2 + half) * rows, 16), rows)]
        dst = rfl.at[z, pl.ds(pl.multiple_of(half * rows, 16), rows)]
        return pltpu.make_async_remote_copy(
            src_ref=src, dst_ref=dst, send_sem=rf_send.at[dz], recv_sem=rf_recv.at[dz],
            device_id=(to * 2 + y, c), device_id_type=MESH)

    def fwd_copy(dz):
        origin = lax.rem(z + zc - dz, zc)
        piece = rfl.at[origin, pl.ds(pl.multiple_of(half * rows, 16), rows)]
        return pltpu.make_async_remote_copy(
            src_ref=piece, dst_ref=piece, send_sem=fwd_send.at[dz], recv_sem=fwd_recv.at[dz],
            device_id=(me, mate), device_id_type=MESH)

    def fwd_arrival(dz):
        origin = lax.rem(z + zc - dz, zc)
        piece = rfl.at[origin, pl.ds(pl.multiple_of((1 - half) * rows, 16), rows)]
        return pltpu.make_async_copy(piece, piece, fwd_recv.at[dz])

    def y_copy(j):
        return pltpu.make_async_remote_copy(
            src_ref=ysend.at[j], dst_ref=yrecv.at[j],
            send_sem=y_send.at[j], recv_sem=y_recv.at[j],
            device_id=(partner, c), device_id_type=MESH)

    for dz in range(1, zc):
        rf_copy(dz).start()
    w_in.start()

    def lhs(which):
        at = pl.ds(pl.multiple_of(which * rows, 16), rows)
        return jnp.concatenate([rfl[o, at, :] for o in range(zc)], axis=1)

    def tick(t, carry):
        @pl.when(t < nch)
        def _():
            own_part = shaped[:, 0:1] * colv[:, chunk(t)].astype(jnp.float32)
            g[t, z, pl.ds(0, mb), :] = own_part.astype(jnp.bfloat16)

            @pl.when(z > 0)
            def _():
                left_copy(0, t).start()

            @pl.when(z < zc - 1)
            def _():
                right_copy(0, t).start()

        @pl.when(t == 0)
        def _():
            if kb > mb:
                g[:, :, pl.ds(mb, kb - mb), :] = jnp.zeros((nch, zc, kb - mb, WIDTH), jnp.bfloat16)
            rfl[z] = rf_ref[pl.ds(pl.multiple_of(z * 2 * rows, 16), 2 * rows), :]

        for d in range(1, zc):
            j = t - d

            @pl.when((j >= 0) & (j < nch))
            def _():
                @pl.when(z + d < zc)
                def _():
                    arrival(z + d, j, left_recv.at[d, j]).wait()
                    if d < zc - 1:
                        @pl.when(z > 0)
                        def _():
                            left_copy(d, j).start()

                @pl.when(z - d >= 0)
                def _():
                    arrival(z - d, j, right_recv.at[d, j]).wait()
                    if d < zc - 1:
                        @pl.when(z < zc - 1)
                        def _():
                            right_copy(d, j).start()

        @pl.when(t == 1)
        def _():
            for dz in range(1, zc):
                rf_copy(dz).wait_recv()
                fwd_copy(dz).start()

        jc = t - (zc - 1)

        @pl.when(jc == 0)
        def _():
            for dz in range(1, zc):
                fwd_arrival(dz).wait()

        @pl.when((jc >= 0) & (jc < nch))
        def _():
            at = chunk(jc)
            rhs = g[jc].reshape(zc * kb, WIDTH)
            ysend[jc] = jnp.dot(lhs(1 - y), rhs, preferred_element_type=jnp.float32).astype(jnp.bfloat16)
            y_copy(jc).start()
            own[:, at] = jnp.dot(lhs(y), rhs, preferred_element_type=jnp.float32)

        jf = jc - LAG

        @pl.when(jf == 0)
        def _():
            w_in.wait()

        @pl.when(jf >= 0)
        def _():
            at = chunk(jf)
            y_copy(jf).wait_recv()
            own[:, at] = wv[:, at] + scale * (own[:, at] + yrecv[jf].astype(jnp.float32))

        return carry

    lax.fori_loop(0, nch + zc - 1 + LAG, tick, 0)

    def drain(j, carry):
        for d in range(zc - 1):
            @pl.when((z + d < zc) & (z > 0))
            def _():
                left_copy(d, j).wait_send()

            @pl.when((z - d >= 0) & (z < zc - 1))
            def _():
                right_copy(d, j).wait_send()
        y_copy(j).wait_send()
        return carry

    lax.fori_loop(0, nch, drain, 0)
    for dz in range(1, zc):
        rf_copy(dz).wait_send()
        fwd_copy(dz).wait_send()


def body(weight, row_factors, col_factors, fitness_ranks):
    pop = lax.axis_size("pop")
    mb = fitness_ranks.shape[0]
    members = mb * pop
    zc = pop // 2
    rows, cols = weight.shape
    kb = -(-mb // 128) * 128
    nch = cols // WIDTH
    anywhere = pl.BlockSpec(memory_space=pl.ANY)
    vmem = pl.BlockSpec(memory_space=pltpu.VMEM)
    dma = pltpu.SemaphoreType.DMA
    return pl.pallas_call(
        functools.partial(kernel, zc, members),
        out_shape=pltpu.VMEM((rows, cols), jnp.float32),
        in_specs=[vmem, vmem, anywhere, anywhere],
        out_specs=vmem,
        scratch_shapes=[
            pltpu.VMEM((mb, 128), jnp.float32),
            pltpu.VMEM((row_factors.shape[0], kb), jnp.bfloat16),
            pltpu.VMEM((mb, cols), jnp.bfloat16),
            pltpu.VMEM((nch, zc, kb, WIDTH), jnp.bfloat16),
            pltpu.VMEM((zc, 2 * rows, kb), jnp.bfloat16),
            pltpu.VMEM((nch, rows, WIDTH), jnp.bfloat16),
            pltpu.VMEM((nch, rows, WIDTH), jnp.bfloat16),
            pltpu.VMEM((rows, cols), jnp.float32),
            dma((2,)),
            dma((zc, nch)), dma((zc, nch)), dma((zc, nch)), dma((zc, nch)),
            dma((zc,)), dma((zc,)), dma((zc,)), dma((zc,)),
            dma((nch,)), dma((nch,)),
        ],
        compiler_params=pltpu.CompilerParams(
            collective_id=0, has_side_effects=True, vmem_limit_bytes=56 * 1024 * 1024),
        cost_estimate=pl.CostEstimate(
            flops=2 * rows * cols * members, bytes_accessed=8 * rows * cols, transcendentals=0),
    )(fitness_ranks.reshape(1, mb), row_factors.T, col_factors, weight)


def solution(mesh):
    in_specs = (P("pop", "col"), P(None, "pop"), P("pop", "col"), P("pop"))
    out_specs = P("pop", "col")
    return jax.shard_map(body, mesh=mesh, in_specs=in_specs, out_specs=out_specs, check_vma=False)
```

```python
import functools
import math

import jax
import jax.numpy as jnp
from jax import lax
from jax.experimental import pallas as pl
from jax.experimental.pallas import tpu as pltpu
from jax.sharding import PartitionSpec as P

MESH = pl.DeviceIdType.MESH
WIDTH = 256
LAG = 2


def kernel(zc, members, ranks_ref, rft_ref, col_ref, w_ref, own,
           shaped, rf_ref, colv, g, rfl, ysend, yrecv, wv, sem_in, left_send, left_recv, right_send, right_recv,
           rf_send, rf_recv, fwd_send, fwd_recv, y_send, y_recv):
    mb, cols = colv.shape
    kb = rf_ref.shape[1]
    rows = own.shape[0]
    nch = cols // WIDTH
    scale = 3.0 / math.sqrt(members)
    me = lax.axis_index("pop")
    c = lax.axis_index("col")
    z, y = me // 2, me % 2
    half = c % 2
    mate = c + 1 - 2 * half
    partner = me + 1 - 2 * y

    col_in = pltpu.make_async_copy(col_ref, colv, sem_in.at[0])
    w_in = pltpu.make_async_copy(w_ref, wv, sem_in.at[1])
    col_in.start()

    barrier = pltpu.get_barrier_semaphore()
    for dz in range(1, zc):
        other = lax.rem(z + dz, zc) * 2 + y
        pl.semaphore_signal(barrier, inc=1, device_id=(other, c), device_id_type=MESH)
    pl.semaphore_signal(barrier, inc=1, device_id=(partner, c), device_id_type=MESH)
    pl.semaphore_signal(barrier, inc=1, device_id=(me, mate), device_id_type=MESH)

    flat = jnp.broadcast_to(ranks_ref[...].astype(jnp.float32), (mb, mb))
    eye = lax.broadcasted_iota(jnp.int32, (mb, mb), 0) == lax.broadcasted_iota(jnp.int32, (mb, mb), 1)
    rank = jnp.sum(jnp.where(eye, flat, 0.0), axis=1, keepdims=True)
    shaped[...] = jnp.broadcast_to(rank / (members - 1) - 0.5, shaped.shape)
    for at in range(0, rf_ref.shape[0], 128):
        part = rft_ref[:, at:at + 128].astype(jnp.float32)
        if kb > mb:
            part = jnp.concatenate([part, jnp.zeros((kb - mb, 128), jnp.float32)], axis=0)
        rf_ref[at:at + 128, :] = part.T.astype(jnp.bfloat16)
    col_in.wait()
    pl.semaphore_wait(barrier, zc + 1)

    def chunk(j):
        return pl.ds(pl.multiple_of(j * WIDTH, WIDTH), WIDTH)

    def block_copy(b, j, send, recv, target):
        piece = g.at[j, b, pl.ds(0, mb), :]
        return pltpu.make_async_remote_copy(
            src_ref=piece, dst_ref=piece, send_sem=send, recv_sem=recv,
            device_id=(target * 2 + y, c), device_id_type=MESH)

    def left_copy(d, j):
        return block_copy(z + d, j, left_send.at[d, j], left_recv.at[d + 1, j], z - 1)

    def right_copy(d, j):
        return block_copy(z - d, j, right_send.at[d, j], right_recv.at[d + 1, j], z + 1)

    def arrival(b, j, recv):
        piece = g.at[j, b, pl.ds(0, mb), :]
        return pltpu.make_async_copy(piece, piece, recv)

    def rf_copy(dz):
        to = lax.rem(z + dz, zc)
        src = rf_ref.at[pl.ds(pl.multiple_of((to * 2 + half) * rows, 16), rows)]
        dst = rfl.at[z, pl.ds(pl.multiple_of(half * rows, 16), rows)]
        return pltpu.make_async_remote_copy(
            src_ref=src, dst_ref=dst, send_sem=rf_send.at[dz], recv_sem=rf_recv.at[dz],
            device_id=(to * 2 + y, c), device_id_type=MESH)

    def fwd_copy(dz):
        origin = lax.rem(z + zc - dz, zc)
        piece = rfl.at[origin, pl.ds(pl.multiple_of(half * rows, 16), rows)]
        return pltpu.make_async_remote_copy(
            src_ref=piece, dst_ref=piece, send_sem=fwd_send.at[dz], recv_sem=fwd_recv.at[dz],
            device_id=(me, mate), device_id_type=MESH)

    def fwd_arrival(dz):
        origin = lax.rem(z + zc - dz, zc)
        piece = rfl.at[origin, pl.ds(pl.multiple_of((1 - half) * rows, 16), rows)]
        return pltpu.make_async_copy(piece, piece, fwd_recv.at[dz])

    def y_copy(j):
        return pltpu.make_async_remote_copy(
            src_ref=ysend.at[j], dst_ref=yrecv.at[j],
            send_sem=y_send.at[j], recv_sem=y_recv.at[j],
            device_id=(partner, c), device_id_type=MESH)

    for dz in range(1, zc):
        rf_copy(dz).start()
    w_in.start()

    def lhs(which):
        at = pl.ds(pl.multiple_of(which * rows, 16), rows)
        return jnp.concatenate([rfl[o, at, :] for o in range(zc)], axis=1)

    def send_own(j):
        own_part = shaped[:, 0:1] * colv[:, chunk(j)].astype(jnp.float32)
        g[j, z, pl.ds(0, mb), :] = own_part.astype(jnp.bfloat16)

        @pl.when(z > 0)
        def _():
            left_copy(0, j).start()

        @pl.when(z < zc - 1)
        def _():
            right_copy(0, j).start()

    send_own(0)

    def tick(t, carry):
        @pl.when(t + 1 < nch)
        def _():
            send_own(t + 1)

        @pl.when(t == 0)
        def _():
            if kb > mb:
                g[:, :, pl.ds(mb, kb - mb), :] = jnp.zeros((nch, zc, kb - mb, WIDTH), jnp.bfloat16)
            rfl[z] = rf_ref[pl.ds(pl.multiple_of(z * 2 * rows, 16), 2 * rows), :]

        for d in range(1, zc):
            j = t - d

            @pl.when((j >= 0) & (j < nch))
            def _():
                @pl.when(z + d < zc)
                def _():
                    arrival(z + d, j, left_recv.at[d, j]).wait()
                    if d < zc - 1:
                        @pl.when(z > 0)
                        def _():
                            left_copy(d, j).start()

                @pl.when(z - d >= 0)
                def _():
                    arrival(z - d, j, right_recv.at[d, j]).wait()
                    if d < zc - 1:
                        @pl.when(z < zc - 1)
                        def _():
                            right_copy(d, j).start()

        @pl.when(t == 1)
        def _():
            for dz in range(1, zc):
                rf_copy(dz).wait_recv()
                fwd_copy(dz).start()

        jc = t - (zc - 1)

        @pl.when(jc == 0)
        def _():
            for dz in range(1, zc):
                fwd_arrival(dz).wait()

        @pl.when((jc >= 0) & (jc < nch))
        def _():
            at = chunk(jc)
            rhs = g[jc].reshape(zc * kb, WIDTH)
            ysend[jc] = jnp.dot(lhs(1 - y), rhs, preferred_element_type=jnp.float32).astype(jnp.bfloat16)
            y_copy(jc).start()
            own[:, at] = jnp.dot(lhs(y), rhs, preferred_element_type=jnp.float32)

        jf = jc - LAG

        @pl.when(jf == 0)
        def _():
            w_in.wait()

        @pl.when(jf >= 0)
        def _():
            at = chunk(jf)
            y_copy(jf).wait_recv()
            own[:, at] = wv[:, at] + scale * (own[:, at] + yrecv[jf].astype(jnp.float32))

        return carry

    lax.fori_loop(0, nch + zc - 1 + LAG, tick, 0)

    def drain(j, carry):
        for d in range(zc - 1):
            @pl.when((z + d < zc) & (z > 0))
            def _():
                left_copy(d, j).wait_send()

            @pl.when((z - d >= 0) & (z < zc - 1))
            def _():
                right_copy(d, j).wait_send()
        y_copy(j).wait_send()
        return carry

    lax.fori_loop(0, nch, drain, 0)
    for dz in range(1, zc):
        rf_copy(dz).wait_send()
        fwd_copy(dz).wait_send()


def body(weight, row_factors, col_factors, fitness_ranks):
    pop = lax.axis_size("pop")
    mb = fitness_ranks.shape[0]
    members = mb * pop
    zc = pop // 2
    rows, cols = weight.shape
    kb = -(-mb // 128) * 128
    nch = cols // WIDTH
    anywhere = pl.BlockSpec(memory_space=pl.ANY)
    vmem = pl.BlockSpec(memory_space=pltpu.VMEM)
    dma = pltpu.SemaphoreType.DMA
    return pl.pallas_call(
        functools.partial(kernel, zc, members),
        out_shape=pltpu.VMEM((rows, cols), jnp.float32),
        in_specs=[vmem, vmem, anywhere, anywhere],
        out_specs=vmem,
        scratch_shapes=[
            pltpu.VMEM((mb, 128), jnp.float32),
            pltpu.VMEM((row_factors.shape[0], kb), jnp.bfloat16),
            pltpu.VMEM((mb, cols), jnp.bfloat16),
            pltpu.VMEM((nch, zc, kb, WIDTH), jnp.bfloat16),
            pltpu.VMEM((zc, 2 * rows, kb), jnp.bfloat16),
            pltpu.VMEM((nch, rows, WIDTH), jnp.bfloat16),
            pltpu.VMEM((nch, rows, WIDTH), jnp.bfloat16),
            pltpu.VMEM((rows, cols), jnp.float32),
            dma((2,)),
            dma((zc, nch)), dma((zc, nch)), dma((zc, nch)), dma((zc, nch)),
            dma((zc,)), dma((zc,)), dma((zc,)), dma((zc,)),
            dma((nch,)), dma((nch,)),
        ],
        compiler_params=pltpu.CompilerParams(
            collective_id=0, has_side_effects=True, vmem_limit_bytes=56 * 1024 * 1024),
        cost_estimate=pl.CostEstimate(
            flops=2 * rows * cols * members, bytes_accessed=8 * rows * cols, transcendentals=0),
    )(fitness_ranks.reshape(1, mb), row_factors.T, col_factors, weight)


def solution(mesh):
    in_specs = (P("pop", "col"), P(None, "pop"), P("pop", "col"), P("pop"))
    out_specs = P("pop", "col")
    return jax.shard_map(body, mesh=mesh, in_specs=in_specs, out_specs=out_specs, check_vma=False)
```

```python
import functools
import math

import jax
import jax.numpy as jnp
from jax import lax
from jax.experimental import pallas as pl
from jax.experimental.pallas import tpu as pltpu
from jax.sharding import PartitionSpec as P

MESH = pl.DeviceIdType.MESH
WIDTH = 128
LAG = 3


def kernel(zc, members, share, ranks_ref, rft_ref, col_ref, w_ref, own,
           shaped, rf_ref, colv, g, rfl, ysend, yrecv, wv, sem_in, left_send, left_recv, right_send, right_recv,
           rf_send, rf_recv, x_send, x_recv, fwd_send, fwd_recv, y_send, y_recv):
    mb, cols = colv.shape
    kb = rf_ref.shape[1]
    rows = own.shape[0]
    nch = cols // WIDTH
    scale = 3.0 / math.sqrt(members)
    me = lax.axis_index("pop")
    c = lax.axis_index("col")
    z, y = me // 2, me % 2
    part = c % share
    piece_rows = 2 * rows // share
    core = c % 2
    mate = c + 1 - 2 * core
    x_mate = c + 2 - 4 * (part // 2)
    partner = me + 1 - 2 * y

    col_in = pltpu.make_async_copy(col_ref, colv, sem_in.at[0])
    w_in = pltpu.make_async_copy(w_ref, wv, sem_in.at[1])
    col_in.start()

    barrier = pltpu.get_barrier_semaphore()
    for dz in range(1, zc):
        other = lax.rem(z + dz, zc) * 2 + y
        pl.semaphore_signal(barrier, inc=1, device_id=(other, c), device_id_type=MESH)
    pl.semaphore_signal(barrier, inc=1, device_id=(partner, c), device_id_type=MESH)
    pl.semaphore_signal(barrier, inc=1, device_id=(me, mate), device_id_type=MESH)
    if share == 4:
        pl.semaphore_signal(barrier, inc=1, device_id=(me, x_mate), device_id_type=MESH)

    flat = jnp.broadcast_to(ranks_ref[...].astype(jnp.float32), (mb, mb))
    eye = lax.broadcasted_iota(jnp.int32, (mb, mb), 0) == lax.broadcasted_iota(jnp.int32, (mb, mb), 1)
    rank = jnp.sum(jnp.where(eye, flat, 0.0), axis=1, keepdims=True)
    shaped[...] = jnp.broadcast_to(rank / (members - 1) - 0.5, shaped.shape)
    for at in range(0, rf_ref.shape[0], 128):
        tile = rft_ref[:, at:at + 128].astype(jnp.float32)
        if kb > mb:
            tile = jnp.concatenate([tile, jnp.zeros((kb - mb, 128), jnp.float32)], axis=0)
        rf_ref[at:at + 128, :] = tile.T.astype(jnp.bfloat16)
    col_in.wait()
    pl.semaphore_wait(barrier, zc + 1 + (share == 4))

    def chunk(j):
        return pl.ds(pl.multiple_of(j * WIDTH, WIDTH), WIDTH)

    def block_copy(b, j, send, recv, target):
        piece = g.at[j, b, pl.ds(0, mb), :]
        return pltpu.make_async_remote_copy(
            src_ref=piece, dst_ref=piece, send_sem=send, recv_sem=recv,
            device_id=(target * 2 + y, c), device_id_type=MESH)

    def left_copy(d, j):
        return block_copy(z + d, j, left_send.at[d, j], left_recv.at[d + 1, j], z - 1)

    def right_copy(d, j):
        return block_copy(z - d, j, right_send.at[d, j], right_recv.at[d + 1, j], z + 1)

    def arrival(b, j, recv):
        piece = g.at[j, b, pl.ds(0, mb), :]
        return pltpu.make_async_copy(piece, piece, recv)

    def rf_rows(index):
        return pl.ds(pl.multiple_of(index * piece_rows, 16), piece_rows)

    def rf_copy(dz):
        to = lax.rem(z + dz, zc)
        return pltpu.make_async_remote_copy(
            src_ref=rf_ref.at[rf_rows(to * share + part)], dst_ref=rfl.at[z, rf_rows(part)],
            send_sem=rf_send.at[dz], recv_sem=rf_recv.at[dz],
            device_id=(to * 2 + y, c), device_id_type=MESH)

    def pass_on(dz, index, send, recv, target):
        piece = rfl.at[lax.rem(z + zc - dz, zc), rf_rows(index)]
        return pltpu.make_async_remote_copy(
            src_ref=piece, dst_ref=piece, send_sem=send, recv_sem=recv,
            device_id=(me, target), device_id_type=MESH)

    def x_copy(dz):
        return pass_on(dz, part, x_send.at[dz], x_recv.at[dz], x_mate)

    def fwd_copy(dz, k):
        index = part if k == 0 else lax.rem(part + 2, share)
        return pass_on(dz, index, fwd_send.at[dz, k], fwd_recv.at[dz, k], mate)

    def landed(dz, index, recv):
        piece = rfl.at[lax.rem(z + zc - dz, zc), rf_rows(index)]
        return pltpu.make_async_copy(piece, piece, recv)

    def y_copy(j):
        return pltpu.make_async_remote_copy(
            src_ref=ysend.at[j], dst_ref=yrecv.at[j],
            send_sem=y_send.at[j], recv_sem=y_recv.at[j],
            device_id=(partner, c), device_id_type=MESH)

    for dz in range(1, zc):
        rf_copy(dz).start()
    w_in.start()

    def lhs(which):
        at = pl.ds(pl.multiple_of(which * rows, 16), rows)
        return jnp.concatenate([rfl[o, at, :] for o in range(zc)], axis=1)

    def tick(t, carry):
        @pl.when(t < nch)
        def _():
            own_part = shaped[:, 0:1] * colv[:, chunk(t)].astype(jnp.float32)
            g[t, z, pl.ds(0, mb), :] = own_part.astype(jnp.bfloat16)

            @pl.when(z > 0)
            def _():
                left_copy(0, t).start()

            @pl.when(z < zc - 1)
            def _():
                right_copy(0, t).start()

        @pl.when(t == 0)
        def _():
            if kb > mb:
                g[:, :, pl.ds(mb, kb - mb), :] = jnp.zeros((nch, zc, kb - mb, WIDTH), jnp.bfloat16)
            rfl[z] = rf_ref[pl.ds(pl.multiple_of(z * 2 * rows, 16), 2 * rows), :]

        for d in range(1, zc):
            j = t - d

            @pl.when((j >= 0) & (j < nch))
            def _():
                @pl.when(z + d < zc)
                def _():
                    arrival(z + d, j, left_recv.at[d, j]).wait()
                    if d < zc - 1:
                        @pl.when(z > 0)
                        def _():
                            left_copy(d, j).start()

                @pl.when(z - d >= 0)
                def _():
                    arrival(z - d, j, right_recv.at[d, j]).wait()
                    if d < zc - 1:
                        @pl.when(z < zc - 1)
                        def _():
                            right_copy(d, j).start()

        @pl.when(t == 1)
        def _():
            for dz in range(1, zc):
                rf_copy(dz).wait_recv()
                if share == 4:
                    x_copy(dz).start()
                fwd_copy(dz, 0).start()

        jc = t - (zc - 1)

        @pl.when(jc == 0)
        def _():
            mate_part = part + 1 - 2 * core
            if share == 4:
                for dz in range(1, zc):
                    landed(dz, lax.rem(part + 2, share), x_recv.at[dz]).wait()
                    fwd_copy(dz, 1).start()
            for dz in range(1, zc):
                landed(dz, mate_part, fwd_recv.at[dz, 0]).wait()
            if share == 4:
                for dz in range(1, zc):
                    landed(dz, lax.rem(mate_part + 2, share), fwd_recv.at[dz, 1]).wait()

        @pl.when((jc >= 0) & (jc < nch))
        def _():
            at = chunk(jc)
            rhs = g[jc].reshape(zc * kb, WIDTH)
            ysend[jc] = jnp.dot(lhs(1 - y), rhs, preferred_element_type=jnp.float32).astype(jnp.bfloat16)
            y_copy(jc).start()
            own[:, at] = jnp.dot(lhs(y), rhs, preferred_element_type=jnp.float32)

        jf = jc - LAG

        @pl.when(jf == 0)
        def _():
            w_in.wait()

        @pl.when(jf >= 0)
        def _():
            at = chunk(jf)
            y_copy(jf).wait_recv()
            own[:, at] = wv[:, at] + scale * (own[:, at] + yrecv[jf].astype(jnp.float32))

        return carry

    lax.fori_loop(0, nch + zc - 1 + LAG, tick, 0)

    def drain(j, carry):
        for d in range(zc - 1):
            @pl.when((z + d < zc) & (z > 0))
            def _():
                left_copy(d, j).wait_send()

            @pl.when((z - d >= 0) & (z < zc - 1))
            def _():
                right_copy(d, j).wait_send()
        y_copy(j).wait_send()
        return carry

    lax.fori_loop(0, nch, drain, 0)
    for dz in range(1, zc):
        rf_copy(dz).wait_send()
        fwd_copy(dz, 0).wait_send()
        if share == 4:
            x_copy(dz).wait_send()
            fwd_copy(dz, 1).wait_send()


def body(weight, row_factors, col_factors, fitness_ranks):
    pop = lax.axis_size("pop")
    mb = fitness_ranks.shape[0]
    members = mb * pop
    zc = pop // 2
    rows, cols = weight.shape
    kb = -(-mb // 128) * 128
    nch = cols // WIDTH
    share = 4 if rows % 32 == 0 and lax.axis_size("col") % 4 == 0 else 2
    anywhere = pl.BlockSpec(memory_space=pl.ANY)
    vmem = pl.BlockSpec(memory_space=pltpu.VMEM)
    dma = pltpu.SemaphoreType.DMA
    return pl.pallas_call(
        functools.partial(kernel, zc, members, share),
        out_shape=pltpu.VMEM((rows, cols), jnp.float32),
        in_specs=[vmem, vmem, anywhere, anywhere],
        out_specs=vmem,
        scratch_shapes=[
            pltpu.VMEM((mb, 128), jnp.float32),
            pltpu.VMEM((row_factors.shape[0], kb), jnp.bfloat16),
            pltpu.VMEM((mb, cols), jnp.bfloat16),
            pltpu.VMEM((nch, zc, kb, WIDTH), jnp.bfloat16),
            pltpu.VMEM((zc, 2 * rows, kb), jnp.bfloat16),
            pltpu.VMEM((nch, rows, WIDTH), jnp.bfloat16),
            pltpu.VMEM((nch, rows, WIDTH), jnp.bfloat16),
            pltpu.VMEM((rows, cols), jnp.float32),
            dma((2,)),
            dma((zc, nch)), dma((zc, nch)), dma((zc, nch)), dma((zc, nch)),
            dma((zc,)), dma((zc,)), dma((zc,)), dma((zc,)), dma((zc, 2)), dma((zc, 2)),
            dma((nch,)), dma((nch,)),
        ],
        compiler_params=pltpu.CompilerParams(
            collective_id=0, has_side_effects=True, vmem_limit_bytes=56 * 1024 * 1024),
        cost_estimate=pl.CostEstimate(
            flops=2 * rows * cols * members, bytes_accessed=8 * rows * cols, transcendentals=0),
    )(fitness_ranks.reshape(1, mb), row_factors.T, col_factors, weight)


def solution(mesh):
    in_specs = (P("pop", "col"), P(None, "pop"), P("pop", "col"), P("pop"))
    out_specs = P("pop", "col")
    return jax.shard_map(body, mesh=mesh, in_specs=in_specs, out_specs=out_specs, check_vma=False)
```

```python
import functools
import math

import jax
import jax.numpy as jnp
from jax import lax
from jax.experimental import pallas as pl
from jax.experimental.pallas import tpu as pltpu
from jax.sharding import PartitionSpec as P

MESH = pl.DeviceIdType.MESH
WIDTH = 256
LAG = 2


def kernel(zc, members, share, ranks_ref, rft_ref, col_ref, w_ref, own,
           shaped, rf_ref, colv, g, rfl, ysend, yrecv, wv, sem_in, left_send, left_recv, right_send, right_recv,
           rf_send, rf_recv, x_send, x_recv, fwd_send, fwd_recv, y_send, y_recv):
    mb, cols = colv.shape
    kb = rf_ref.shape[1]
    rows = own.shape[0]
    nch = cols // WIDTH
    scale = 3.0 / math.sqrt(members)
    me = lax.axis_index("pop")
    c = lax.axis_index("col")
    z, y = me // 2, me % 2
    part = c % share
    piece_rows = 2 * rows // share
    core = c % 2
    mate = c + 1 - 2 * core
    x_mate = c + 2 - 4 * (part // 2)
    partner = me + 1 - 2 * y

    col_in = pltpu.make_async_copy(col_ref, colv, sem_in.at[0])
    w_in = pltpu.make_async_copy(w_ref, wv, sem_in.at[1])
    col_in.start()

    barrier = pltpu.get_barrier_semaphore()
    for dz in range(1, zc):
        other = lax.rem(z + dz, zc) * 2 + y
        pl.semaphore_signal(barrier, inc=1, device_id=(other, c), device_id_type=MESH)
    pl.semaphore_signal(barrier, inc=1, device_id=(partner, c), device_id_type=MESH)
    pl.semaphore_signal(barrier, inc=1, device_id=(me, mate), device_id_type=MESH)
    if share == 4:
        pl.semaphore_signal(barrier, inc=1, device_id=(me, x_mate), device_id_type=MESH)

    flat = jnp.broadcast_to(ranks_ref[...].astype(jnp.float32), (mb, mb))
    eye = lax.broadcasted_iota(jnp.int32, (mb, mb), 0) == lax.broadcasted_iota(jnp.int32, (mb, mb), 1)
    rank = jnp.sum(jnp.where(eye, flat, 0.0), axis=1, keepdims=True)
    shaped[...] = jnp.broadcast_to(rank / (members - 1) - 0.5, shaped.shape)
    for at in range(0, rf_ref.shape[0], 128):
        tile = rft_ref[:, at:at + 128].astype(jnp.float32)
        if kb > mb:
            tile = jnp.concatenate([tile, jnp.zeros((kb - mb, 128), jnp.float32)], axis=0)
        rf_ref[at:at + 128, :] = tile.T.astype(jnp.bfloat16)
    col_in.wait()
    pl.semaphore_wait(barrier, zc + 1 + (share == 4))

    def chunk(j):
        return pl.ds(pl.multiple_of(j * WIDTH, WIDTH), WIDTH)

    def block_copy(b, j, send, recv, target):
        piece = g.at[j, b, pl.ds(0, mb), :]
        return pltpu.make_async_remote_copy(
            src_ref=piece, dst_ref=piece, send_sem=send, recv_sem=recv,
            device_id=(target * 2 + y, c), device_id_type=MESH)

    def left_copy(d, j):
        return block_copy(z + d, j, left_send.at[d, j], left_recv.at[d + 1, j], z - 1)

    def right_copy(d, j):
        return block_copy(z - d, j, right_send.at[d, j], right_recv.at[d + 1, j], z + 1)

    def arrival(b, j, recv):
        piece = g.at[j, b, pl.ds(0, mb), :]
        return pltpu.make_async_copy(piece, piece, recv)

    def rf_rows(index):
        return pl.ds(pl.multiple_of(index * piece_rows, 16), piece_rows)

    def rf_copy(dz):
        to = lax.rem(z + dz, zc)
        return pltpu.make_async_remote_copy(
            src_ref=rf_ref.at[rf_rows(to * share + part)], dst_ref=rfl.at[z, rf_rows(part)],
            send_sem=rf_send.at[dz], recv_sem=rf_recv.at[dz],
            device_id=(to * 2 + y, c), device_id_type=MESH)

    def pass_on(dz, index, send, recv, target):
        piece = rfl.at[lax.rem(z + zc - dz, zc), rf_rows(index)]
        return pltpu.make_async_remote_copy(
            src_ref=piece, dst_ref=piece, send_sem=send, recv_sem=recv,
            device_id=(me, target), device_id_type=MESH)

    def x_copy(dz):
        return pass_on(dz, part, x_send.at[dz], x_recv.at[dz], x_mate)

    def fwd_copy(dz, k):
        index = part if k == 0 else lax.rem(part + 2, share)
        return pass_on(dz, index, fwd_send.at[dz, k], fwd_recv.at[dz, k], mate)

    def landed(dz, index, recv):
        piece = rfl.at[lax.rem(z + zc - dz, zc), rf_rows(index)]
        return pltpu.make_async_copy(piece, piece, recv)

    def y_copy(j):
        return pltpu.make_async_remote_copy(
            src_ref=ysend.at[j], dst_ref=yrecv.at[j],
            send_sem=y_send.at[j], recv_sem=y_recv.at[j],
            device_id=(partner, c), device_id_type=MESH)

    for dz in range(1, zc):
        rf_copy(dz).start()
    w_in.start()

    def lhs(which):
        at = pl.ds(pl.multiple_of(which * rows, 16), rows)
        return jnp.concatenate([rfl[o, at, :] for o in range(zc)], axis=1)

    def tick(t, carry):
        @pl.when(t < nch)
        def _():
            own_part = shaped[:, 0:1] * colv[:, chunk(t)].astype(jnp.float32)
            g[t, z, pl.ds(0, mb), :] = own_part.astype(jnp.bfloat16)

            @pl.when(z > 0)
            def _():
                left_copy(0, t).start()

            @pl.when(z < zc - 1)
            def _():
                right_copy(0, t).start()

        @pl.when(t == 0)
        def _():
            if kb > mb:
                g[:, :, pl.ds(mb, kb - mb), :] = jnp.zeros((nch, zc, kb - mb, WIDTH), jnp.bfloat16)
            rfl[z] = rf_ref[pl.ds(pl.multiple_of(z * 2 * rows, 16), 2 * rows), :]

        for d in range(1, zc):
            j = t - d

            @pl.when((j >= 0) & (j < nch))
            def _():
                @pl.when(z + d < zc)
                def _():
                    arrival(z + d, j, left_recv.at[d, j]).wait()
                    if d < zc - 1:
                        @pl.when(z > 0)
                        def _():
                            left_copy(d, j).start()

                @pl.when(z - d >= 0)
                def _():
                    arrival(z - d, j, right_recv.at[d, j]).wait()
                    if d < zc - 1:
                        @pl.when(z < zc - 1)
                        def _():
                            right_copy(d, j).start()

        @pl.when(t == 1)
        def _():
            for dz in range(1, zc):
                rf_copy(dz).wait_recv()
                if share == 4:
                    x_copy(dz).start()
                fwd_copy(dz, 0).start()

        jc = t - (zc - 1)

        @pl.when(jc == 0)
        def _():
            mate_part = part + 1 - 2 * core
            if share == 4:
                for dz in range(1, zc):
                    landed(dz, lax.rem(part + 2, share), x_recv.at[dz]).wait()
                    fwd_copy(dz, 1).start()
            for dz in range(1, zc):
                landed(dz, mate_part, fwd_recv.at[dz, 0]).wait()
            if share == 4:
                for dz in range(1, zc):
                    landed(dz, lax.rem(mate_part + 2, share), fwd_recv.at[dz, 1]).wait()

        @pl.when((jc >= 0) & (jc < nch))
        def _():
            at = chunk(jc)
            rhs = g[jc].reshape(zc * kb, WIDTH)
            ysend[jc] = jnp.dot(lhs(1 - y), rhs, preferred_element_type=jnp.float32).astype(jnp.bfloat16)
            y_copy(jc).start()
            own[:, at] = jnp.dot(lhs(y), rhs, preferred_element_type=jnp.float32)

        jf = jc - LAG

        @pl.when(jf == 0)
        def _():
            w_in.wait()

        @pl.when(jf >= 0)
        def _():
            at = chunk(jf)
            y_copy(jf).wait_recv()
            own[:, at] = wv[:, at] + scale * (own[:, at] + yrecv[jf].astype(jnp.float32))

        return carry

    lax.fori_loop(0, nch + zc - 1 + LAG, tick, 0)

    def drain(j, carry):
        for d in range(zc - 1):
            @pl.when((z + d < zc) & (z > 0))
            def _():
                left_copy(d, j).wait_send()

            @pl.when((z - d >= 0) & (z < zc - 1))
            def _():
                right_copy(d, j).wait_send()
        y_copy(j).wait_send()
        return carry

    lax.fori_loop(0, nch, drain, 0)
    for dz in range(1, zc):
        rf_copy(dz).wait_send()
        fwd_copy(dz, 0).wait_send()
        if share == 4:
            x_copy(dz).wait_send()
            fwd_copy(dz, 1).wait_send()


def body(weight, row_factors, col_factors, fitness_ranks):
    pop = lax.axis_size("pop")
    mb = fitness_ranks.shape[0]
    members = mb * pop
    zc = pop // 2
    rows, cols = weight.shape
    kb = -(-mb // 128) * 128
    nch = cols // WIDTH
    share = 4 if rows % 32 == 0 and lax.axis_size("col") % 4 == 0 else 2
    anywhere = pl.BlockSpec(memory_space=pl.ANY)
    vmem = pl.BlockSpec(memory_space=pltpu.VMEM)
    dma = pltpu.SemaphoreType.DMA
    return pl.pallas_call(
        functools.partial(kernel, zc, members, share),
        out_shape=pltpu.VMEM((rows, cols), jnp.float32),
        in_specs=[vmem, vmem, anywhere, anywhere],
        out_specs=vmem,
        scratch_shapes=[
            pltpu.VMEM((mb, 128), jnp.float32),
            pltpu.VMEM((row_factors.shape[0], kb), jnp.bfloat16),
            pltpu.VMEM((mb, cols), jnp.bfloat16),
            pltpu.VMEM((nch, zc, kb, WIDTH), jnp.bfloat16),
            pltpu.VMEM((zc, 2 * rows, kb), jnp.bfloat16),
            pltpu.VMEM((nch, rows, WIDTH), jnp.bfloat16),
            pltpu.VMEM((nch, rows, WIDTH), jnp.bfloat16),
            pltpu.VMEM((rows, cols), jnp.float32),
            dma((2,)),
            dma((zc, nch)), dma((zc, nch)), dma((zc, nch)), dma((zc, nch)),
            dma((zc,)), dma((zc,)), dma((zc,)), dma((zc,)), dma((zc, 2)), dma((zc, 2)),
            dma((nch,)), dma((nch,)),
        ],
        compiler_params=pltpu.CompilerParams(
            collective_id=0, has_side_effects=True, vmem_limit_bytes=56 * 1024 * 1024),
        cost_estimate=pl.CostEstimate(
            flops=2 * rows * cols * members, bytes_accessed=8 * rows * cols, transcendentals=0),
    )(fitness_ranks.reshape(1, mb), row_factors.T, col_factors, weight)


def solution(mesh):
    in_specs = (P("pop", "col"), P(None, "pop"), P("pop", "col"), P("pop"))
    out_specs = P("pop", "col")
    return jax.shard_map(body, mesh=mesh, in_specs=in_specs, out_specs=out_specs, check_vma=False)
```

```python
import functools
import math

import jax
import jax.numpy as jnp
from jax import lax
from jax.experimental import pallas as pl
from jax.experimental.pallas import tpu as pltpu
from jax.sharding import PartitionSpec as P

MESH = pl.DeviceIdType.MESH
WIDTH = 256
LAG = 2


def kernel(zc, members, share, ranks_ref, rft_ref, col_ref, w_ref, own,
           shaped, rf_ref, colv, g, rfl, ysend, yrecv, wv, sem_in, left_send, left_recv, right_send, right_recv,
           rf_send, rf_recv, x_send, x_recv, fwd_send, fwd_recv, y_send, y_recv):
    mb, cols = colv.shape
    kb = rf_ref.shape[1]
    rows = own.shape[0]
    nch = cols // WIDTH + 1
    scale = 3.0 / math.sqrt(members)
    me = lax.axis_index("pop")
    c = lax.axis_index("col")
    z, y = me // 2, me % 2
    part = c % share
    piece_rows = 2 * rows // share
    core = c % 2
    mate = c + 1 - 2 * core
    x_mate = c + 2 - 4 * (part // 2)
    partner = me + 1 - 2 * y

    col_in = pltpu.make_async_copy(col_ref, colv, sem_in.at[0])
    w_in = pltpu.make_async_copy(w_ref, wv, sem_in.at[1])
    col_in.start()

    barrier = pltpu.get_barrier_semaphore()
    for dz in range(1, zc):
        other = lax.rem(z + dz, zc) * 2 + y
        pl.semaphore_signal(barrier, inc=1, device_id=(other, c), device_id_type=MESH)
    pl.semaphore_signal(barrier, inc=1, device_id=(partner, c), device_id_type=MESH)
    pl.semaphore_signal(barrier, inc=1, device_id=(me, mate), device_id_type=MESH)
    if share == 4:
        pl.semaphore_signal(barrier, inc=1, device_id=(me, x_mate), device_id_type=MESH)

    flat = jnp.broadcast_to(ranks_ref[...].astype(jnp.float32), (mb, mb))
    eye = lax.broadcasted_iota(jnp.int32, (mb, mb), 0) == lax.broadcasted_iota(jnp.int32, (mb, mb), 1)
    rank = jnp.sum(jnp.where(eye, flat, 0.0), axis=1, keepdims=True)
    shaped[...] = jnp.broadcast_to(rank / (members - 1) - 0.5, shaped.shape)
    for at in range(0, rf_ref.shape[0], 128):
        tile = rft_ref[:, at:at + 128].astype(jnp.float32)
        if kb > mb:
            tile = jnp.concatenate([tile, jnp.zeros((kb - mb, 128), jnp.float32)], axis=0)
        rf_ref[at:at + 128, :] = tile.T.astype(jnp.bfloat16)
    col_in.wait()
    pl.semaphore_wait(barrier, zc + 1 + (share == 4))

    def either(j, action):
        edge = (j == 0) | (j == nch - 1)

        @pl.when(edge)
        def _():
            action(j, WIDTH // 2)

        @pl.when(jnp.logical_not(edge))
        def _():
            action(j, WIDTH)

    def chunk(j, width):
        start = jnp.maximum(j * WIDTH - WIDTH // 2, 0)
        return pl.ds(pl.multiple_of(start, WIDTH // 2), width)

    def block_copy(b, j, width, send, recv, target):
        piece = g.at[j, b, pl.ds(0, mb), pl.ds(0, width)]
        return pltpu.make_async_remote_copy(
            src_ref=piece, dst_ref=piece, send_sem=send, recv_sem=recv,
            device_id=(target * 2 + y, c), device_id_type=MESH)

    def left_copy(d, j, width):
        return block_copy(z + d, j, width, left_send.at[d, j], left_recv.at[d + 1, j], z - 1)

    def right_copy(d, j, width):
        return block_copy(z - d, j, width, right_send.at[d, j], right_recv.at[d + 1, j], z + 1)

    def arrival(b, j, width, recv):
        piece = g.at[j, b, pl.ds(0, mb), pl.ds(0, width)]
        return pltpu.make_async_copy(piece, piece, recv)

    def rf_rows(index):
        return pl.ds(pl.multiple_of(index * piece_rows, 16), piece_rows)

    def rf_copy(dz):
        to = lax.rem(z + dz, zc)
        return pltpu.make_async_remote_copy(
            src_ref=rf_ref.at[rf_rows(to * share + part)], dst_ref=rfl.at[z, rf_rows(part)],
            send_sem=rf_send.at[dz], recv_sem=rf_recv.at[dz],
            device_id=(to * 2 + y, c), device_id_type=MESH)

    def pass_on(dz, index, send, recv, target):
        piece = rfl.at[lax.rem(z + zc - dz, zc), rf_rows(index)]
        return pltpu.make_async_remote_copy(
            src_ref=piece, dst_ref=piece, send_sem=send, recv_sem=recv,
            device_id=(me, target), device_id_type=MESH)

    def x_copy(dz):
        return pass_on(dz, part, x_send.at[dz], x_recv.at[dz], x_mate)

    def fwd_copy(dz, k):
        index = part if k == 0 else lax.rem(part + 2, share)
        return pass_on(dz, index, fwd_send.at[dz, k], fwd_recv.at[dz, k], mate)

    def landed(dz, index, recv):
        piece = rfl.at[lax.rem(z + zc - dz, zc), rf_rows(index)]
        return pltpu.make_async_copy(piece, piece, recv)

    def y_copy(j, width):
        at = (j, slice(None), pl.ds(0, width))
        return pltpu.make_async_remote_copy(
            src_ref=ysend.at[at], dst_ref=yrecv.at[at],
            send_sem=y_send.at[j], recv_sem=y_recv.at[j],
            device_id=(partner, c), device_id_type=MESH)

    for dz in range(1, zc):
        rf_copy(dz).start()
    w_in.start()

    def lhs(which):
        at = pl.ds(pl.multiple_of(which * rows, 16), rows)
        return jnp.concatenate([rfl[o, at, :] for o in range(zc)], axis=1)

    def send_own(j, width):
        own_part = shaped[:, 0:1] * colv[:, chunk(j, width)].astype(jnp.float32)
        g[j, z, pl.ds(0, mb), pl.ds(0, width)] = own_part.astype(jnp.bfloat16)

        @pl.when(z > 0)
        def _():
            left_copy(0, j, width).start()

        @pl.when(z < zc - 1)
        def _():
            right_copy(0, j, width).start()

    def hop(d):
        def action(j, width):
            @pl.when(z + d < zc)
            def _():
                arrival(z + d, j, width, left_recv.at[d, j]).wait()
                if d < zc - 1:
                    @pl.when(z > 0)
                    def _():
                        left_copy(d, j, width).start()

            @pl.when(z - d >= 0)
            def _():
                arrival(z - d, j, width, right_recv.at[d, j]).wait()
                if d < zc - 1:
                    @pl.when(z < zc - 1)
                    def _():
                        right_copy(d, j, width).start()
        return action

    def multiply(j, width):
        rhs = g[j, :, :, pl.ds(0, width)].reshape(zc * kb, width)
        other = jnp.dot(lhs(1 - y), rhs, preferred_element_type=jnp.float32)
        ysend[j, :, pl.ds(0, width)] = other.astype(jnp.bfloat16)
        y_copy(j, width).start()
        own[:, chunk(j, width)] = jnp.dot(lhs(y), rhs, preferred_element_type=jnp.float32)

    def finish(j, width):
        at = chunk(j, width)
        y_copy(j, width).wait_recv()
        own[:, at] = wv[:, at] + scale * (own[:, at] + yrecv[j, :, pl.ds(0, width)].astype(jnp.float32))

    def tick(t, carry):
        @pl.when(t < nch)
        def _():
            either(t, send_own)

        @pl.when(t == 0)
        def _():
            if kb > mb:
                g[:, :, pl.ds(mb, kb - mb), :] = jnp.zeros((nch, zc, kb - mb, WIDTH), jnp.bfloat16)
            rfl[z] = rf_ref[pl.ds(pl.multiple_of(z * 2 * rows, 16), 2 * rows), :]

        for d in range(1, zc):
            j = t - d

            @pl.when((j >= 0) & (j < nch))
            def _():
                either(j, hop(d))

        @pl.when(t == 1)
        def _():
            for dz in range(1, zc):
                rf_copy(dz).wait_recv()
                if share == 4:
                    x_copy(dz).start()
                fwd_copy(dz, 0).start()

        jc = t - (zc - 1)

        @pl.when(jc == 0)
        def _():
            mate_part = part + 1 - 2 * core
            if share == 4:
                for dz in range(1, zc):
                    landed(dz, lax.rem(part + 2, share), x_recv.at[dz]).wait()
                    fwd_copy(dz, 1).start()
            for dz in range(1, zc):
                landed(dz, mate_part, fwd_recv.at[dz, 0]).wait()
            if share == 4:
                for dz in range(1, zc):
                    landed(dz, lax.rem(mate_part + 2, share), fwd_recv.at[dz, 1]).wait()

        @pl.when((jc >= 0) & (jc < nch))
        def _():
            either(jc, multiply)

        jf = jc - LAG

        @pl.when(jf == 0)
        def _():
            w_in.wait()

        @pl.when(jf >= 0)
        def _():
            either(jf, finish)

        return carry

    lax.fori_loop(0, nch + zc - 1 + LAG, tick, 0)

    def sent(j, width):
        for d in range(zc - 1):
            @pl.when((z + d < zc) & (z > 0))
            def _():
                left_copy(d, j, width).wait_send()

            @pl.when((z - d >= 0) & (z < zc - 1))
            def _():
                right_copy(d, j, width).wait_send()
        y_copy(j, width).wait_send()

    def drain(j, carry):
        either(j, sent)
        return carry

    lax.fori_loop(0, nch, drain, 0)
    for dz in range(1, zc):
        rf_copy(dz).wait_send()
        fwd_copy(dz, 0).wait_send()
        if share == 4:
            x_copy(dz).wait_send()
            fwd_copy(dz, 1).wait_send()


def body(weight, row_factors, col_factors, fitness_ranks):
    pop = lax.axis_size("pop")
    mb = fitness_ranks.shape[0]
    members = mb * pop
    zc = pop // 2
    rows, cols = weight.shape
    kb = -(-mb // 128) * 128
    nch = cols // WIDTH + 1
    share = 4 if rows % 32 == 0 and lax.axis_size("col") % 4 == 0 else 2
    anywhere = pl.BlockSpec(memory_space=pl.ANY)
    vmem = pl.BlockSpec(memory_space=pltpu.VMEM)
    dma = pltpu.SemaphoreType.DMA
    return pl.pallas_call(
        functools.partial(kernel, zc, members, share),
        out_shape=pltpu.VMEM((rows, cols), jnp.float32),
        in_specs=[vmem, vmem, anywhere, anywhere],
        out_specs=vmem,
        scratch_shapes=[
            pltpu.VMEM((mb, 128), jnp.float32),
            pltpu.VMEM((row_factors.shape[0], kb), jnp.bfloat16),
            pltpu.VMEM((mb, cols), jnp.bfloat16),
            pltpu.VMEM((nch, zc, kb, WIDTH), jnp.bfloat16),
            pltpu.VMEM((zc, 2 * rows, kb), jnp.bfloat16),
            pltpu.VMEM((nch, rows, WIDTH), jnp.bfloat16),
            pltpu.VMEM((nch, rows, WIDTH), jnp.bfloat16),
            pltpu.VMEM((rows, cols), jnp.float32),
            dma((2,)),
            dma((zc, nch)), dma((zc, nch)), dma((zc, nch)), dma((zc, nch)),
            dma((zc,)), dma((zc,)), dma((zc,)), dma((zc,)), dma((zc, 2)), dma((zc, 2)),
            dma((nch,)), dma((nch,)),
        ],
        compiler_params=pltpu.CompilerParams(
            collective_id=0, has_side_effects=True, vmem_limit_bytes=56 * 1024 * 1024),
        cost_estimate=pl.CostEstimate(
            flops=2 * rows * cols * members, bytes_accessed=8 * rows * cols, transcendentals=0),
    )(fitness_ranks.reshape(1, mb), row_factors.T, col_factors, weight)


def solution(mesh):
    in_specs = (P("pop", "col"), P(None, "pop"), P("pop", "col"), P("pop"))
    out_specs = P("pop", "col")
    return jax.shard_map(body, mesh=mesh, in_specs=in_specs, out_specs=out_specs, check_vma=False)
```

```python
import functools
import math

import jax
import jax.numpy as jnp
from jax import lax
from jax.experimental import pallas as pl
from jax.experimental.pallas import tpu as pltpu
from jax.sharding import PartitionSpec as P

MESH = pl.DeviceIdType.MESH
WIDTH = 512
LAG = 2


def kernel(zc, members, share, ranks_ref, rft_ref, col_ref, w_ref, own,
           shaped, rf_ref, colv, g, rfl, ysend, yrecv, wv, sem_in, left_send, left_recv, right_send, right_recv,
           rf_send, rf_recv, x_send, x_recv, fwd_send, fwd_recv, y_send, y_recv):
    mb, cols = colv.shape
    kb = rf_ref.shape[1]
    rows = own.shape[0]
    nch = cols // WIDTH + 1
    scale = 3.0 / math.sqrt(members)
    me = lax.axis_index("pop")
    c = lax.axis_index("col")
    z, y = me // 2, me % 2
    part = c % share
    piece_rows = 2 * rows // share
    core = c % 2
    mate = c + 1 - 2 * core
    x_mate = c + 2 - 4 * (part // 2)
    partner = me + 1 - 2 * y

    col_in = pltpu.make_async_copy(col_ref, colv, sem_in.at[0])
    w_in = pltpu.make_async_copy(w_ref, wv, sem_in.at[1])
    col_in.start()

    barrier = pltpu.get_barrier_semaphore()
    for dz in range(1, zc):
        other = lax.rem(z + dz, zc) * 2 + y
        pl.semaphore_signal(barrier, inc=1, device_id=(other, c), device_id_type=MESH)
    pl.semaphore_signal(barrier, inc=1, device_id=(partner, c), device_id_type=MESH)
    pl.semaphore_signal(barrier, inc=1, device_id=(me, mate), device_id_type=MESH)
    if share == 4:
        pl.semaphore_signal(barrier, inc=1, device_id=(me, x_mate), device_id_type=MESH)

    flat = jnp.broadcast_to(ranks_ref[...].astype(jnp.float32), (mb, mb))
    eye = lax.broadcasted_iota(jnp.int32, (mb, mb), 0) == lax.broadcasted_iota(jnp.int32, (mb, mb), 1)
    rank = jnp.sum(jnp.where(eye, flat, 0.0), axis=1, keepdims=True)
    shaped[...] = jnp.broadcast_to(rank / (members - 1) - 0.5, shaped.shape)
    for at in range(0, rf_ref.shape[0], 128):
        tile = rft_ref[:, at:at + 128].astype(jnp.float32)
        if kb > mb:
            tile = jnp.concatenate([tile, jnp.zeros((kb - mb, 128), jnp.float32)], axis=0)
        rf_ref[at:at + 128, :] = tile.T.astype(jnp.bfloat16)
    col_in.wait()
    pl.semaphore_wait(barrier, zc + 1 + (share == 4))

    def either(j, action):
        edge = (j == 0) | (j == nch - 1)

        @pl.when(edge)
        def _():
            action(j, WIDTH // 2)

        @pl.when(jnp.logical_not(edge))
        def _():
            action(j, WIDTH)

    def chunk(j, width):
        start = jnp.maximum(j * WIDTH - WIDTH // 2, 0)
        return pl.ds(pl.multiple_of(start, WIDTH // 2), width)

    def block_copy(b, j, width, send, recv, target):
        piece = g.at[j, b, pl.ds(0, mb), pl.ds(0, width)]
        return pltpu.make_async_remote_copy(
            src_ref=piece, dst_ref=piece, send_sem=send, recv_sem=recv,
            device_id=(target * 2 + y, c), device_id_type=MESH)

    def left_copy(d, j, width):
        return block_copy(z + d, j, width, left_send.at[d, j], left_recv.at[d + 1, j], z - 1)

    def right_copy(d, j, width):
        return block_copy(z - d, j, width, right_send.at[d, j], right_recv.at[d + 1, j], z + 1)

    def arrival(b, j, width, recv):
        piece = g.at[j, b, pl.ds(0, mb), pl.ds(0, width)]
        return pltpu.make_async_copy(piece, piece, recv)

    def rf_rows(index):
        return pl.ds(pl.multiple_of(index * piece_rows, 16), piece_rows)

    def rf_copy(dz):
        to = lax.rem(z + dz, zc)
        return pltpu.make_async_remote_copy(
            src_ref=rf_ref.at[rf_rows(to * share + part)], dst_ref=rfl.at[z, rf_rows(part)],
            send_sem=rf_send.at[dz], recv_sem=rf_recv.at[dz],
            device_id=(to * 2 + y, c), device_id_type=MESH)

    def pass_on(dz, index, send, recv, target):
        piece = rfl.at[lax.rem(z + zc - dz, zc), rf_rows(index)]
        return pltpu.make_async_remote_copy(
            src_ref=piece, dst_ref=piece, send_sem=send, recv_sem=recv,
            device_id=(me, target), device_id_type=MESH)

    def x_copy(dz):
        return pass_on(dz, part, x_send.at[dz], x_recv.at[dz], x_mate)

    def fwd_copy(dz, k):
        index = part if k == 0 else lax.rem(part + 2, share)
        return pass_on(dz, index, fwd_send.at[dz, k], fwd_recv.at[dz, k], mate)

    def landed(dz, index, recv):
        piece = rfl.at[lax.rem(z + zc - dz, zc), rf_rows(index)]
        return pltpu.make_async_copy(piece, piece, recv)

    def y_copy(j, width):
        at = (j, slice(None), pl.ds(0, width))
        return pltpu.make_async_remote_copy(
            src_ref=ysend.at[at], dst_ref=yrecv.at[at],
            send_sem=y_send.at[j], recv_sem=y_recv.at[j],
            device_id=(partner, c), device_id_type=MESH)

    for dz in range(1, zc):
        rf_copy(dz).start()
    w_in.start()

    def lhs(which):
        at = pl.ds(pl.multiple_of(which * rows, 16), rows)
        return jnp.concatenate([rfl[o, at, :] for o in range(zc)], axis=1)

    def send_own(j, width):
        own_part = shaped[:, 0:1] * colv[:, chunk(j, width)].astype(jnp.float32)
        g[j, z, pl.ds(0, mb), pl.ds(0, width)] = own_part.astype(jnp.bfloat16)

        @pl.when(z > 0)
        def _():
            left_copy(0, j, width).start()

        @pl.when(z < zc - 1)
        def _():
            right_copy(0, j, width).start()

    def hop(d):
        def action(j, width):
            @pl.when(z + d < zc)
            def _():
                arrival(z + d, j, width, left_recv.at[d, j]).wait()
                if d < zc - 1:
                    @pl.when(z > 0)
                    def _():
                        left_copy(d, j, width).start()

            @pl.when(z - d >= 0)
            def _():
                arrival(z - d, j, width, right_recv.at[d, j]).wait()
                if d < zc - 1:
                    @pl.when(z < zc - 1)
                    def _():
                        right_copy(d, j, width).start()
        return action

    def multiply(j, width):
        rhs = g[j, :, :, pl.ds(0, width)].reshape(zc * kb, width)
        other = jnp.dot(lhs(1 - y), rhs, preferred_element_type=jnp.float32)
        ysend[j, :, pl.ds(0, width)] = other.astype(jnp.bfloat16)
        y_copy(j, width).start()
        own[:, chunk(j, width)] = jnp.dot(lhs(y), rhs, preferred_element_type=jnp.float32)

    def finish(j, width):
        at = chunk(j, width)
        y_copy(j, width).wait_recv()
        own[:, at] = wv[:, at] + scale * (own[:, at] + yrecv[j, :, pl.ds(0, width)].astype(jnp.float32))

    def tick(t, carry):
        @pl.when(t < nch)
        def _():
            either(t, send_own)

        @pl.when(t == 0)
        def _():
            if kb > mb:
                g[:, :, pl.ds(mb, kb - mb), :] = jnp.zeros((nch, zc, kb - mb, WIDTH), jnp.bfloat16)
            rfl[z] = rf_ref[pl.ds(pl.multiple_of(z * 2 * rows, 16), 2 * rows), :]

        for d in range(1, zc):
            j = t - d

            @pl.when((j >= 0) & (j < nch))
            def _():
                either(j, hop(d))

        @pl.when(t == 1)
        def _():
            for dz in range(1, zc):
                rf_copy(dz).wait_recv()
                if share == 4:
                    x_copy(dz).start()
                fwd_copy(dz, 0).start()

        jc = t - (zc - 1)

        @pl.when(jc == 0)
        def _():
            mate_part = part + 1 - 2 * core
            if share == 4:
                for dz in range(1, zc):
                    landed(dz, lax.rem(part + 2, share), x_recv.at[dz]).wait()
                    fwd_copy(dz, 1).start()
            for dz in range(1, zc):
                landed(dz, mate_part, fwd_recv.at[dz, 0]).wait()
            if share == 4:
                for dz in range(1, zc):
                    landed(dz, lax.rem(mate_part + 2, share), fwd_recv.at[dz, 1]).wait()

        @pl.when((jc >= 0) & (jc < nch))
        def _():
            either(jc, multiply)

        jf = jc - LAG

        @pl.when(jf == 0)
        def _():
            w_in.wait()

        @pl.when(jf >= 0)
        def _():
            either(jf, finish)

        return carry

    lax.fori_loop(0, nch + zc - 1 + LAG, tick, 0)

    def sent(j, width):
        for d in range(zc - 1):
            @pl.when((z + d < zc) & (z > 0))
            def _():
                left_copy(d, j, width).wait_send()

            @pl.when((z - d >= 0) & (z < zc - 1))
            def _():
                right_copy(d, j, width).wait_send()
        y_copy(j, width).wait_send()

    def drain(j, carry):
        either(j, sent)
        return carry

    lax.fori_loop(0, nch, drain, 0)
    for dz in range(1, zc):
        rf_copy(dz).wait_send()
        fwd_copy(dz, 0).wait_send()
        if share == 4:
            x_copy(dz).wait_send()
            fwd_copy(dz, 1).wait_send()


def body(weight, row_factors, col_factors, fitness_ranks):
    pop = lax.axis_size("pop")
    mb = fitness_ranks.shape[0]
    members = mb * pop
    zc = pop // 2
    rows, cols = weight.shape
    kb = -(-mb // 128) * 128
    nch = cols // WIDTH + 1
    share = 4 if rows % 32 == 0 and lax.axis_size("col") % 4 == 0 else 2
    anywhere = pl.BlockSpec(memory_space=pl.ANY)
    vmem = pl.BlockSpec(memory_space=pltpu.VMEM)
    dma = pltpu.SemaphoreType.DMA
    return pl.pallas_call(
        functools.partial(kernel, zc, members, share),
        out_shape=pltpu.VMEM((rows, cols), jnp.float32),
        in_specs=[vmem, vmem, anywhere, anywhere],
        out_specs=vmem,
        scratch_shapes=[
            pltpu.VMEM((mb, 128), jnp.float32),
            pltpu.VMEM((row_factors.shape[0], kb), jnp.bfloat16),
            pltpu.VMEM((mb, cols), jnp.bfloat16),
            pltpu.VMEM((nch, zc, kb, WIDTH), jnp.bfloat16),
            pltpu.VMEM((zc, 2 * rows, kb), jnp.bfloat16),
            pltpu.VMEM((nch, rows, WIDTH), jnp.bfloat16),
            pltpu.VMEM((nch, rows, WIDTH), jnp.bfloat16),
            pltpu.VMEM((rows, cols), jnp.float32),
            dma((2,)),
            dma((zc, nch)), dma((zc, nch)), dma((zc, nch)), dma((zc, nch)),
            dma((zc,)), dma((zc,)), dma((zc,)), dma((zc,)), dma((zc, 2)), dma((zc, 2)),
            dma((nch,)), dma((nch,)),
        ],
        compiler_params=pltpu.CompilerParams(
            collective_id=0, has_side_effects=True, vmem_limit_bytes=56 * 1024 * 1024),
        cost_estimate=pl.CostEstimate(
            flops=2 * rows * cols * members, bytes_accessed=8 * rows * cols, transcendentals=0),
    )(fitness_ranks.reshape(1, mb), row_factors.T, col_factors, weight)


def solution(mesh):
    in_specs = (P("pop", "col"), P(None, "pop"), P("pop", "col"), P("pop"))
    out_specs = P("pop", "col")
    return jax.shard_map(body, mesh=mesh, in_specs=in_specs, out_specs=out_specs, check_vma=False)
```

```python
import functools
import math

import jax
import jax.numpy as jnp
from jax import lax
from jax.experimental import pallas as pl
from jax.experimental.pallas import tpu as pltpu
from jax.sharding import PartitionSpec as P

MESH = pl.DeviceIdType.MESH
WIDTH = 512
LAG = 2


def kernel(zc, members, share, ranks_ref, rft_ref, col_ref, w_ref, own,
           shaped, rf_ref, colv, g, rfl, ysend, yrecv, wv, sem_in, left_send, left_recv, right_send, right_recv,
           rf_send, rf_recv, x_send, x_recv, fwd_send, fwd_recv, y_send, y_recv):
    mb, cols = colv.shape
    kb = rf_ref.shape[1]
    rows = own.shape[0]
    nch = cols // WIDTH + 3
    scale = 3.0 / math.sqrt(members)
    me = lax.axis_index("pop")
    c = lax.axis_index("col")
    z, y = me // 2, me % 2
    part = c % share
    piece_rows = 2 * rows // share
    core = c % 2
    mate = c + 1 - 2 * core
    x_mate = c + 2 - 4 * (part // 2)
    partner = me + 1 - 2 * y

    col_in = pltpu.make_async_copy(col_ref, colv, sem_in.at[0])
    w_in = pltpu.make_async_copy(w_ref, wv, sem_in.at[1])
    col_in.start()

    barrier = pltpu.get_barrier_semaphore()
    for dz in range(1, zc):
        other = lax.rem(z + dz, zc) * 2 + y
        pl.semaphore_signal(barrier, inc=1, device_id=(other, c), device_id_type=MESH)
    pl.semaphore_signal(barrier, inc=1, device_id=(partner, c), device_id_type=MESH)
    pl.semaphore_signal(barrier, inc=1, device_id=(me, mate), device_id_type=MESH)
    if share == 4:
        pl.semaphore_signal(barrier, inc=1, device_id=(me, x_mate), device_id_type=MESH)

    flat = jnp.broadcast_to(ranks_ref[...].astype(jnp.float32), (mb, mb))
    eye = lax.broadcasted_iota(jnp.int32, (mb, mb), 0) == lax.broadcasted_iota(jnp.int32, (mb, mb), 1)
    rank = jnp.sum(jnp.where(eye, flat, 0.0), axis=1, keepdims=True)
    shaped[...] = jnp.broadcast_to(rank / (members - 1) - 0.5, shaped.shape)
    for at in range(0, rf_ref.shape[0], 128):
        tile = rft_ref[:, at:at + 128].astype(jnp.float32)
        if kb > mb:
            tile = jnp.concatenate([tile, jnp.zeros((kb - mb, 128), jnp.float32)], axis=0)
        rf_ref[at:at + 128, :] = tile.T.astype(jnp.bfloat16)
    col_in.wait()
    pl.semaphore_wait(barrier, zc + 1 + (share == 4))

    def either(j, action):
        quarter = (j == 0) | (j == nch - 1)
        half = (j == 1) | (j == nch - 2) | (j == nch - 3)

        @pl.when(quarter)
        def _():
            action(j, WIDTH // 4)

        @pl.when(half)
        def _():
            action(j, WIDTH // 2)

        @pl.when(jnp.logical_not(quarter | half))
        def _():
            action(j, WIDTH)

    def chunk(j, width):
        full = jnp.clip(j - 2, 0, nch - 5)
        start = (WIDTH // 4 * jnp.minimum(j, 1) + WIDTH // 2 * jnp.clip(j - 1, 0, 1)
                 + WIDTH * full + WIDTH // 2 * jnp.maximum(j - (nch - 3), 0))
        return pl.ds(pl.multiple_of(start, WIDTH // 4), width)

    def block_copy(b, j, width, send, recv, target):
        piece = g.at[j, b, pl.ds(0, mb), pl.ds(0, width)]
        return pltpu.make_async_remote_copy(
            src_ref=piece, dst_ref=piece, send_sem=send, recv_sem=recv,
            device_id=(target * 2 + y, c), device_id_type=MESH)

    def left_copy(d, j, width):
        return block_copy(z + d, j, width, left_send.at[d, j], left_recv.at[d + 1, j], z - 1)

    def right_copy(d, j, width):
        return block_copy(z - d, j, width, right_send.at[d, j], right_recv.at[d + 1, j], z + 1)

    def arrival(b, j, width, recv):
        piece = g.at[j, b, pl.ds(0, mb), pl.ds(0, width)]
        return pltpu.make_async_copy(piece, piece, recv)

    def rf_rows(index):
        return pl.ds(pl.multiple_of(index * piece_rows, 16), piece_rows)

    def rf_copy(dz):
        to = lax.rem(z + dz, zc)
        return pltpu.make_async_remote_copy(
            src_ref=rf_ref.at[rf_rows(to * share + part)], dst_ref=rfl.at[z, rf_rows(part)],
            send_sem=rf_send.at[dz], recv_sem=rf_recv.at[dz],
            device_id=(to * 2 + y, c), device_id_type=MESH)

    def pass_on(dz, index, send, recv, target):
        piece = rfl.at[lax.rem(z + zc - dz, zc), rf_rows(index)]
        return pltpu.make_async_remote_copy(
            src_ref=piece, dst_ref=piece, send_sem=send, recv_sem=recv,
            device_id=(me, target), device_id_type=MESH)

    def x_copy(dz):
        return pass_on(dz, part, x_send.at[dz], x_recv.at[dz], x_mate)

    def fwd_copy(dz, k):
        index = part if k == 0 else lax.rem(part + 2, share)
        return pass_on(dz, index, fwd_send.at[dz, k], fwd_recv.at[dz, k], mate)

    def landed(dz, index, recv):
        piece = rfl.at[lax.rem(z + zc - dz, zc), rf_rows(index)]
        return pltpu.make_async_copy(piece, piece, recv)

    def y_copy(j, width):
        at = (j, slice(None), pl.ds(0, width))
        return pltpu.make_async_remote_copy(
            src_ref=ysend.at[at], dst_ref=yrecv.at[at],
            send_sem=y_send.at[j], recv_sem=y_recv.at[j],
            device_id=(partner, c), device_id_type=MESH)

    for dz in range(1, zc):
        rf_copy(dz).start()
    w_in.start()

    def lhs(which):
        at = pl.ds(pl.multiple_of(which * rows, 16), rows)
        return jnp.concatenate([rfl[o, at, :] for o in range(zc)], axis=1)

    def send_own(j, width):
        own_part = shaped[:, 0:1] * colv[:, chunk(j, width)].astype(jnp.float32)
        g[j, z, pl.ds(0, mb), pl.ds(0, width)] = own_part.astype(jnp.bfloat16)

        @pl.when(z > 0)
        def _():
            left_copy(0, j, width).start()

        @pl.when(z < zc - 1)
        def _():
            right_copy(0, j, width).start()

    def hop(d):
        def action(j, width):
            @pl.when(z + d < zc)
            def _():
                arrival(z + d, j, width, left_recv.at[d, j]).wait()
                if d < zc - 1:
                    @pl.when(z > 0)
                    def _():
                        left_copy(d, j, width).start()

            @pl.when(z - d >= 0)
            def _():
                arrival(z - d, j, width, right_recv.at[d, j]).wait()
                if d < zc - 1:
                    @pl.when(z < zc - 1)
                    def _():
                        right_copy(d, j, width).start()
        return action

    def multiply(j, width):
        rhs = g[j, :, :, pl.ds(0, width)].reshape(zc * kb, width)
        other = jnp.dot(lhs(1 - y), rhs, preferred_element_type=jnp.float32)
        ysend[j, :, pl.ds(0, width)] = other.astype(jnp.bfloat16)
        y_copy(j, width).start()
        own[:, chunk(j, width)] = jnp.dot(lhs(y), rhs, preferred_element_type=jnp.float32)

    def finish(j, width):
        at = chunk(j, width)
        y_copy(j, width).wait_recv()
        own[:, at] = wv[:, at] + scale * (own[:, at] + yrecv[j, :, pl.ds(0, width)].astype(jnp.float32))

    def tick(t, carry):
        @pl.when(t < nch)
        def _():
            either(t, send_own)

        @pl.when(t == 0)
        def _():
            if kb > mb:
                g[:, :, pl.ds(mb, kb - mb), :] = jnp.zeros((nch, zc, kb - mb, WIDTH), jnp.bfloat16)
            rfl[z] = rf_ref[pl.ds(pl.multiple_of(z * 2 * rows, 16), 2 * rows), :]

        for d in range(1, zc):
            j = t - d

            @pl.when((j >= 0) & (j < nch))
            def _():
                either(j, hop(d))

        @pl.when(t == 1)
        def _():
            for dz in range(1, zc):
                rf_copy(dz).wait_recv()
                if share == 4:
                    x_copy(dz).start()
                fwd_copy(dz, 0).start()

        jc = t - (zc - 1)

        @pl.when(jc == 0)
        def _():
            mate_part = part + 1 - 2 * core
            if share == 4:
                for dz in range(1, zc):
                    landed(dz, lax.rem(part + 2, share), x_recv.at[dz]).wait()
                    fwd_copy(dz, 1).start()
            for dz in range(1, zc):
                landed(dz, mate_part, fwd_recv.at[dz, 0]).wait()
            if share == 4:
                for dz in range(1, zc):
                    landed(dz, lax.rem(mate_part + 2, share), fwd_recv.at[dz, 1]).wait()

        @pl.when((jc >= 0) & (jc < nch))
        def _():
            either(jc, multiply)

        jf = jc - LAG

        @pl.when(jf == 0)
        def _():
            w_in.wait()

        @pl.when(jf >= 0)
        def _():
            either(jf, finish)

        return carry

    lax.fori_loop(0, nch + zc - 1 + LAG, tick, 0)

    def sent(j, width):
        for d in range(zc - 1):
            @pl.when((z + d < zc) & (z > 0))
            def _():
                left_copy(d, j, width).wait_send()

            @pl.when((z - d >= 0) & (z < zc - 1))
            def _():
                right_copy(d, j, width).wait_send()
        y_copy(j, width).wait_send()

    def drain(j, carry):
        either(j, sent)
        return carry

    lax.fori_loop(0, nch, drain, 0)
    for dz in range(1, zc):
        rf_copy(dz).wait_send()
        fwd_copy(dz, 0).wait_send()
        if share == 4:
            x_copy(dz).wait_send()
            fwd_copy(dz, 1).wait_send()


def body(weight, row_factors, col_factors, fitness_ranks):
    pop = lax.axis_size("pop")
    mb = fitness_ranks.shape[0]
    members = mb * pop
    zc = pop // 2
    rows, cols = weight.shape
    kb = -(-mb // 128) * 128
    nch = cols // WIDTH + 3
    share = 4 if rows % 32 == 0 and lax.axis_size("col") % 4 == 0 else 2
    anywhere = pl.BlockSpec(memory_space=pl.ANY)
    vmem = pl.BlockSpec(memory_space=pltpu.VMEM)
    dma = pltpu.SemaphoreType.DMA
    return pl.pallas_call(
        functools.partial(kernel, zc, members, share),
        out_shape=pltpu.VMEM((rows, cols), jnp.float32),
        in_specs=[vmem, vmem, anywhere, anywhere],
        out_specs=vmem,
        scratch_shapes=[
            pltpu.VMEM((mb, 128), jnp.float32),
            pltpu.VMEM((row_factors.shape[0], kb), jnp.bfloat16),
            pltpu.VMEM((mb, cols), jnp.bfloat16),
            pltpu.VMEM((nch, zc, kb, WIDTH), jnp.bfloat16),
            pltpu.VMEM((zc, 2 * rows, kb), jnp.bfloat16),
            pltpu.VMEM((nch, rows, WIDTH), jnp.bfloat16),
            pltpu.VMEM((nch, rows, WIDTH), jnp.bfloat16),
            pltpu.VMEM((rows, cols), jnp.float32),
            dma((2,)),
            dma((zc, nch)), dma((zc, nch)), dma((zc, nch)), dma((zc, nch)),
            dma((zc,)), dma((zc,)), dma((zc,)), dma((zc,)), dma((zc, 2)), dma((zc, 2)),
            dma((nch,)), dma((nch,)),
        ],
        compiler_params=pltpu.CompilerParams(
            collective_id=0, has_side_effects=True, vmem_limit_bytes=56 * 1024 * 1024),
        cost_estimate=pl.CostEstimate(
            flops=2 * rows * cols * members, bytes_accessed=8 * rows * cols, transcendentals=0),
    )(fitness_ranks.reshape(1, mb), row_factors.T, col_factors, weight)


def solution(mesh):
    in_specs = (P("pop", "col"), P(None, "pop"), P("pop", "col"), P("pop"))
    out_specs = P("pop", "col")
    return jax.shard_map(body, mesh=mesh, in_specs=in_specs, out_specs=out_specs, check_vma=False)
```

```python
import functools
import math

import jax
import jax.numpy as jnp
from jax import lax
from jax.experimental import pallas as pl
from jax.experimental.pallas import tpu as pltpu
from jax.sharding import PartitionSpec as P

MESH = pl.DeviceIdType.MESH
WIDTH = 256
LAG = 5


def kernel(zc, members, share, ranks_ref, rft_ref, col_ref, w_ref, own,
           shaped, rf_ref, colv, g, rfl, ysend, yrecv, wv, sem_in, left_send, left_recv, right_send, right_recv,
           rf_send, rf_recv, x_send, x_recv, fwd_send, fwd_recv, y_send, y_recv):
    mb, cols = colv.shape
    kb = rf_ref.shape[1]
    rows = own.shape[0]
    nch = cols // WIDTH + 1
    scale = 3.0 / math.sqrt(members)
    me = lax.axis_index("pop")
    c = lax.axis_index("col")
    z, y = me // 2, me % 2
    part = c % share
    piece_rows = 2 * rows // share
    core = c % 2
    mate = c + 1 - 2 * core
    x_mate = c + 2 - 4 * (part // 2)
    partner = me + 1 - 2 * y

    col_in = pltpu.make_async_copy(col_ref, colv, sem_in.at[0])
    w_in = pltpu.make_async_copy(w_ref, wv, sem_in.at[1])
    col_in.start()

    barrier = pltpu.get_barrier_semaphore()
    for dz in range(1, zc):
        other = lax.rem(z + dz, zc) * 2 + y
        pl.semaphore_signal(barrier, inc=1, device_id=(other, c), device_id_type=MESH)
    pl.semaphore_signal(barrier, inc=1, device_id=(partner, c), device_id_type=MESH)
    pl.semaphore_signal(barrier, inc=1, device_id=(me, mate), device_id_type=MESH)
    if share == 4:
        pl.semaphore_signal(barrier, inc=1, device_id=(me, x_mate), device_id_type=MESH)

    flat = jnp.broadcast_to(ranks_ref[...].astype(jnp.float32), (mb, mb))
    eye = lax.broadcasted_iota(jnp.int32, (mb, mb), 0) == lax.broadcasted_iota(jnp.int32, (mb, mb), 1)
    rank = jnp.sum(jnp.where(eye, flat, 0.0), axis=1, keepdims=True)
    shaped[...] = jnp.broadcast_to(rank / (members - 1) - 0.5, shaped.shape)
    for at in range(0, rf_ref.shape[0], 128):
        tile = rft_ref[:, at:at + 128].astype(jnp.float32)
        if kb > mb:
            tile = jnp.concatenate([tile, jnp.zeros((kb - mb, 128), jnp.float32)], axis=0)
        rf_ref[at:at + 128, :] = tile.T.astype(jnp.bfloat16)
    col_in.wait()
    pl.semaphore_wait(barrier, zc + 1 + (share == 4))

    def either(j, action):
        edge = (j == 0) | (j == nch - 1)

        @pl.when(edge)
        def _():
            action(j, WIDTH // 2)

        @pl.when(jnp.logical_not(edge))
        def _():
            action(j, WIDTH)

    def chunk(j, width):
        start = jnp.maximum(j * WIDTH - WIDTH // 2, 0)
        return pl.ds(pl.multiple_of(start, WIDTH // 2), width)

    def block_copy(b, j, width, send, recv, target):
        piece = g.at[j, b, pl.ds(0, mb), pl.ds(0, width)]
        return pltpu.make_async_remote_copy(
            src_ref=piece, dst_ref=piece, send_sem=send, recv_sem=recv,
            device_id=(target * 2 + y, c), device_id_type=MESH)

    def left_copy(d, j, width):
        return block_copy(z + d, j, width, left_send.at[d, j], left_recv.at[d + 1, j], z - 1)

    def right_copy(d, j, width):
        return block_copy(z - d, j, width, right_send.at[d, j], right_recv.at[d + 1, j], z + 1)

    def arrival(b, j, width, recv):
        piece = g.at[j, b, pl.ds(0, mb), pl.ds(0, width)]
        return pltpu.make_async_copy(piece, piece, recv)

    def rf_rows(index):
        return pl.ds(pl.multiple_of(index * piece_rows, 16), piece_rows)

    def rf_copy(dz):
        to = lax.rem(z + dz, zc)
        return pltpu.make_async_remote_copy(
            src_ref=rf_ref.at[rf_rows(to * share + part)], dst_ref=rfl.at[z, rf_rows(part)],
            send_sem=rf_send.at[dz], recv_sem=rf_recv.at[dz],
            device_id=(to * 2 + y, c), device_id_type=MESH)

    def pass_on(dz, index, send, recv, target):
        piece = rfl.at[lax.rem(z + zc - dz, zc), rf_rows(index)]
        return pltpu.make_async_remote_copy(
            src_ref=piece, dst_ref=piece, send_sem=send, recv_sem=recv,
            device_id=(me, target), device_id_type=MESH)

    def x_copy(dz):
        return pass_on(dz, part, x_send.at[dz], x_recv.at[dz], x_mate)

    def fwd_copy(dz, k):
        index = part if k == 0 else lax.rem(part + 2, share)
        return pass_on(dz, index, fwd_send.at[dz, k], fwd_recv.at[dz, k], mate)

    def landed(dz, index, recv):
        piece = rfl.at[lax.rem(z + zc - dz, zc), rf_rows(index)]
        return pltpu.make_async_copy(piece, piece, recv)

    def y_copy(j, width):
        at = (j, slice(None), pl.ds(0, width))
        return pltpu.make_async_remote_copy(
            src_ref=ysend.at[at], dst_ref=yrecv.at[at],
            send_sem=y_send.at[j], recv_sem=y_recv.at[j],
            device_id=(partner, c), device_id_type=MESH)

    for dz in range(1, zc):
        rf_copy(dz).start()
    w_in.start()

    def lhs(which):
        at = pl.ds(pl.multiple_of(which * rows, 16), rows)
        return jnp.concatenate([rfl[o, at, :] for o in range(zc)], axis=1)

    def send_own(j, width):
        own_part = shaped[:, 0:1] * colv[:, chunk(j, width)].astype(jnp.float32)
        g[j, z, pl.ds(0, mb), pl.ds(0, width)] = own_part.astype(jnp.bfloat16)

        @pl.when(z > 0)
        def _():
            left_copy(0, j, width).start()

        @pl.when(z < zc - 1)
        def _():
            right_copy(0, j, width).start()

    def hop(d):
        def action(j, width):
            @pl.when(z + d < zc)
            def _():
                arrival(z + d, j, width, left_recv.at[d, j]).wait()
                if d < zc - 1:
                    @pl.when(z > 0)
                    def _():
                        left_copy(d, j, width).start()

            @pl.when(z - d >= 0)
            def _():
                arrival(z - d, j, width, right_recv.at[d, j]).wait()
                if d < zc - 1:
                    @pl.when(z < zc - 1)
                    def _():
                        right_copy(d, j, width).start()
        return action

    def multiply(j, width):
        rhs = g[j, :, :, pl.ds(0, width)].reshape(zc * kb, width)
        other = jnp.dot(lhs(1 - y), rhs, preferred_element_type=jnp.float32)
        ysend[j, :, pl.ds(0, width)] = other.astype(jnp.bfloat16)
        y_copy(j, width).start()
        own[:, chunk(j, width)] = jnp.dot(lhs(y), rhs, preferred_element_type=jnp.float32)

    def finish(j, width):
        at = chunk(j, width)
        y_copy(j, width).wait_recv()
        own[:, at] = wv[:, at] + scale * (own[:, at] + yrecv[j, :, pl.ds(0, width)].astype(jnp.float32))

    def tick(t, carry):
        @pl.when(t < nch)
        def _():
            either(t, send_own)

        @pl.when(t == 0)
        def _():
            if kb > mb:
                g[:, :, pl.ds(mb, kb - mb), :] = jnp.zeros((nch, zc, kb - mb, WIDTH), jnp.bfloat16)
            rfl[z] = rf_ref[pl.ds(pl.multiple_of(z * 2 * rows, 16), 2 * rows), :]

        for d in range(1, zc):
            j = t - d

            @pl.when((j >= 0) & (j < nch))
            def _():
                either(j, hop(d))

        @pl.when(t == 1)
        def _():
            for dz in range(1, zc):
                rf_copy(dz).wait_recv()
                if share == 4:
                    x_copy(dz).start()
                fwd_copy(dz, 0).start()

        jc = t - (zc - 1)

        @pl.when(jc == 0)
        def _():
            mate_part = part + 1 - 2 * core
            if share == 4:
                for dz in range(1, zc):
                    landed(dz, lax.rem(part + 2, share), x_recv.at[dz]).wait()
                    fwd_copy(dz, 1).start()
            for dz in range(1, zc):
                landed(dz, mate_part, fwd_recv.at[dz, 0]).wait()
            if share == 4:
                for dz in range(1, zc):
                    landed(dz, lax.rem(mate_part + 2, share), fwd_recv.at[dz, 1]).wait()

        @pl.when((jc >= 0) & (jc < nch))
        def _():
            either(jc, multiply)

        jf = jc - LAG

        @pl.when(jf == 0)
        def _():
            w_in.wait()

        @pl.when(jf >= 0)
        def _():
            either(jf, finish)

        return carry

    lax.fori_loop(0, nch + zc - 1 + LAG, tick, 0)

    def sent(j, width):
        for d in range(zc - 1):
            @pl.when((z + d < zc) & (z > 0))
            def _():
                left_copy(d, j, width).wait_send()

            @pl.when((z - d >= 0) & (z < zc - 1))
            def _():
                right_copy(d, j, width).wait_send()
        y_copy(j, width).wait_send()

    def drain(j, carry):
        either(j, sent)
        return carry

    lax.fori_loop(0, nch, drain, 0)
    for dz in range(1, zc):
        rf_copy(dz).wait_send()
        fwd_copy(dz, 0).wait_send()
        if share == 4:
            x_copy(dz).wait_send()
            fwd_copy(dz, 1).wait_send()


def body(weight, row_factors, col_factors, fitness_ranks):
    pop = lax.axis_size("pop")
    mb = fitness_ranks.shape[0]
    members = mb * pop
    zc = pop // 2
    rows, cols = weight.shape
    kb = -(-mb // 128) * 128
    nch = cols // WIDTH + 1
    share = 4 if rows % 32 == 0 and lax.axis_size("col") % 4 == 0 else 2
    anywhere = pl.BlockSpec(memory_space=pl.ANY)
    vmem = pl.BlockSpec(memory_space=pltpu.VMEM)
    dma = pltpu.SemaphoreType.DMA
    return pl.pallas_call(
        functools.partial(kernel, zc, members, share),
        out_shape=pltpu.VMEM((rows, cols), jnp.float32),
        in_specs=[vmem, vmem, anywhere, anywhere],
        out_specs=vmem,
        scratch_shapes=[
            pltpu.VMEM((mb, 128), jnp.float32),
            pltpu.VMEM((row_factors.shape[0], kb), jnp.bfloat16),
            pltpu.VMEM((mb, cols), jnp.bfloat16),
            pltpu.VMEM((nch, zc, kb, WIDTH), jnp.bfloat16),
            pltpu.VMEM((zc, 2 * rows, kb), jnp.bfloat16),
            pltpu.VMEM((nch, rows, WIDTH), jnp.bfloat16),
            pltpu.VMEM((nch, rows, WIDTH), jnp.bfloat16),
            pltpu.VMEM((rows, cols), jnp.float32),
            dma((2,)),
            dma((zc, nch)), dma((zc, nch)), dma((zc, nch)), dma((zc, nch)),
            dma((zc,)), dma((zc,)), dma((zc,)), dma((zc,)), dma((zc, 2)), dma((zc, 2)),
            dma((nch,)), dma((nch,)),
        ],
        compiler_params=pltpu.CompilerParams(
            collective_id=0, has_side_effects=True, vmem_limit_bytes=56 * 1024 * 1024),
        cost_estimate=pl.CostEstimate(
            flops=2 * rows * cols * members, bytes_accessed=8 * rows * cols, transcendentals=0),
    )(fitness_ranks.reshape(1, mb), row_factors.T, col_factors, weight)


def solution(mesh):
    in_specs = (P("pop", "col"), P(None, "pop"), P("pop", "col"), P("pop"))
    out_specs = P("pop", "col")
    return jax.shard_map(body, mesh=mesh, in_specs=in_specs, out_specs=out_specs, check_vma=False)
```

```python
import functools
import math

import jax
import jax.numpy as jnp
from jax import lax
from jax.experimental import pallas as pl
from jax.experimental.pallas import tpu as pltpu
from jax.sharding import PartitionSpec as P

MESH = pl.DeviceIdType.MESH
WIDTH = 256
LAG = 2


def kernel(zc, members, share, ranks_ref, rft_ref, col_ref, w_ref, own,
           shaped, rf_ref, colv, g, rfl, ysend, yrecv, wv, sem_in, left_send, left_recv, right_send, right_recv,
           rf_send, rf_recv, x_send, x_recv, fwd_send, fwd_recv, y_send, y_recv):
    mb, cols = colv.shape
    kb = rf_ref.shape[1]
    rows = own.shape[0]
    nch = cols // WIDTH + 1
    scale = 3.0 / math.sqrt(members)
    me = lax.axis_index("pop")
    c = lax.axis_index("col")
    z, y = me // 2, me % 2
    part = c % share
    piece_rows = 2 * rows // share
    core = c % 2
    mate = c + 1 - 2 * core
    x_mate = c + 2 - 4 * (part // 2)
    partner = me + 1 - 2 * y

    col_in = pltpu.make_async_copy(col_ref, colv, sem_in.at[0])
    w_in = pltpu.make_async_copy(w_ref, wv, sem_in.at[1])
    col_in.start()

    barrier = pltpu.get_barrier_semaphore()
    for dz in range(1, zc):
        other = lax.rem(z + dz, zc) * 2 + y
        pl.semaphore_signal(barrier, inc=1, device_id=(other, c), device_id_type=MESH)
    pl.semaphore_signal(barrier, inc=1, device_id=(partner, c), device_id_type=MESH)
    pl.semaphore_signal(barrier, inc=1, device_id=(me, mate), device_id_type=MESH)
    if share == 4:
        pl.semaphore_signal(barrier, inc=1, device_id=(me, x_mate), device_id_type=MESH)

    flat = jnp.broadcast_to(ranks_ref[...].astype(jnp.float32), (mb, mb))
    eye = lax.broadcasted_iota(jnp.int32, (mb, mb), 0) == lax.broadcasted_iota(jnp.int32, (mb, mb), 1)
    rank = jnp.sum(jnp.where(eye, flat, 0.0), axis=1, keepdims=True)
    shaped[...] = jnp.broadcast_to(rank / (members - 1) - 0.5, shaped.shape)
    col_in.wait()
    pl.semaphore_wait(barrier, zc + 1 + (share == 4))

    def either(j, action):
        edge = (j == 0) | (j == nch - 1)

        @pl.when(edge)
        def _():
            action(j, WIDTH // 2)

        @pl.when(jnp.logical_not(edge))
        def _():
            action(j, WIDTH)

    def chunk(j, width):
        start = jnp.maximum(j * WIDTH - WIDTH // 2, 0)
        return pl.ds(pl.multiple_of(start, WIDTH // 2), width)

    def block_copy(b, j, width, send, recv, target):
        piece = g.at[j, b, pl.ds(0, mb), pl.ds(0, width)]
        return pltpu.make_async_remote_copy(
            src_ref=piece, dst_ref=piece, send_sem=send, recv_sem=recv,
            device_id=(target * 2 + y, c), device_id_type=MESH)

    def left_copy(d, j, width):
        return block_copy(z + d, j, width, left_send.at[d, j], left_recv.at[d + 1, j], z - 1)

    def right_copy(d, j, width):
        return block_copy(z - d, j, width, right_send.at[d, j], right_recv.at[d + 1, j], z + 1)

    def arrival(b, j, width, recv):
        piece = g.at[j, b, pl.ds(0, mb), pl.ds(0, width)]
        return pltpu.make_async_copy(piece, piece, recv)

    def rf_rows(index):
        return pl.ds(pl.multiple_of(index * piece_rows, 16), piece_rows)

    def rf_copy(dz):
        to = lax.rem(z + dz, zc)
        return pltpu.make_async_remote_copy(
            src_ref=rf_ref.at[rf_rows(to * share + part)], dst_ref=rfl.at[z, rf_rows(part)],
            send_sem=rf_send.at[dz], recv_sem=rf_recv.at[dz],
            device_id=(to * 2 + y, c), device_id_type=MESH)

    def pass_on(dz, index, send, recv, target):
        piece = rfl.at[lax.rem(z + zc - dz, zc), rf_rows(index)]
        return pltpu.make_async_remote_copy(
            src_ref=piece, dst_ref=piece, send_sem=send, recv_sem=recv,
            device_id=(me, target), device_id_type=MESH)

    def x_copy(dz):
        return pass_on(dz, part, x_send.at[dz], x_recv.at[dz], x_mate)

    def fwd_copy(dz, k):
        index = part if k == 0 else lax.rem(part + 2, share)
        return pass_on(dz, index, fwd_send.at[dz, k], fwd_recv.at[dz, k], mate)

    def landed(dz, index, recv):
        piece = rfl.at[lax.rem(z + zc - dz, zc), rf_rows(index)]
        return pltpu.make_async_copy(piece, piece, recv)

    def y_copy(j, width):
        at = (j, slice(None), pl.ds(0, width))
        return pltpu.make_async_remote_copy(
            src_ref=ysend.at[at], dst_ref=yrecv.at[at],
            send_sem=y_send.at[j], recv_sem=y_recv.at[j],
            device_id=(partner, c), device_id_type=MESH)

    def lhs(which):
        at = pl.ds(pl.multiple_of(which * rows, 16), rows)
        return jnp.concatenate([rfl[o, at, :] for o in range(zc)], axis=1)

    def send_own(j, width):
        own_part = shaped[:, 0:1] * colv[:, chunk(j, width)].astype(jnp.float32)
        g[j, z, pl.ds(0, mb), pl.ds(0, width)] = own_part.astype(jnp.bfloat16)

        @pl.when(z > 0)
        def _():
            left_copy(0, j, width).start()

        @pl.when(z < zc - 1)
        def _():
            right_copy(0, j, width).start()

    def hop(d):
        def action(j, width):
            @pl.when(z + d < zc)
            def _():
                arrival(z + d, j, width, left_recv.at[d, j]).wait()
                if d < zc - 1:
                    @pl.when(z > 0)
                    def _():
                        left_copy(d, j, width).start()

            @pl.when(z - d >= 0)
            def _():
                arrival(z - d, j, width, right_recv.at[d, j]).wait()
                if d < zc - 1:
                    @pl.when(z < zc - 1)
                    def _():
                        right_copy(d, j, width).start()
        return action

    def multiply(j, width):
        rhs = g[j, :, :, pl.ds(0, width)].reshape(zc * kb, width)
        other = jnp.dot(lhs(1 - y), rhs, preferred_element_type=jnp.float32)
        ysend[j, :, pl.ds(0, width)] = other.astype(jnp.bfloat16)
        y_copy(j, width).start()
        own[:, chunk(j, width)] = jnp.dot(lhs(y), rhs, preferred_element_type=jnp.float32)

    def finish(j, width):
        at = chunk(j, width)
        y_copy(j, width).wait_recv()
        own[:, at] = wv[:, at] + scale * (own[:, at] + yrecv[j, :, pl.ds(0, width)].astype(jnp.float32))

    def tick(t, carry):
        @pl.when(t + 1 < nch)
        def _():
            either(t + 1, send_own)

        @pl.when(t == 0)
        def _():
            if kb > mb:
                g[:, :, pl.ds(mb, kb - mb), :] = jnp.zeros((nch, zc, kb - mb, WIDTH), jnp.bfloat16)
            rfl[z] = rf_ref[pl.ds(pl.multiple_of(z * 2 * rows, 16), 2 * rows), :]

        for d in range(1, zc):
            j = t - d

            @pl.when((j >= 0) & (j < nch))
            def _():
                either(j, hop(d))

        @pl.when(t == 1)
        def _():
            for dz in range(1, zc):
                rf_copy(dz).wait_recv()
                if share == 4:
                    x_copy(dz).start()
                fwd_copy(dz, 0).start()

        jc = t - (zc - 1)

        @pl.when(jc == 0)
        def _():
            mate_part = part + 1 - 2 * core
            if share == 4:
                for dz in range(1, zc):
                    landed(dz, lax.rem(part + 2, share), x_recv.at[dz]).wait()
                    fwd_copy(dz, 1).start()
            for dz in range(1, zc):
                landed(dz, mate_part, fwd_recv.at[dz, 0]).wait()
            if share == 4:
                for dz in range(1, zc):
                    landed(dz, lax.rem(mate_part + 2, share), fwd_recv.at[dz, 1]).wait()

        @pl.when((jc >= 0) & (jc < nch))
        def _():
            either(jc, multiply)

        jf = jc - LAG

        @pl.when(jf == 0)
        def _():
            w_in.wait()

        @pl.when(jf >= 0)
        def _():
            either(jf, finish)

        return carry

    send_own(0, WIDTH // 2)
    for at in range(0, rf_ref.shape[0], 128):
        tile = rft_ref[:, at:at + 128].astype(jnp.float32)
        if kb > mb:
            tile = jnp.concatenate([tile, jnp.zeros((kb - mb, 128), jnp.float32)], axis=0)
        rf_ref[at:at + 128, :] = tile.T.astype(jnp.bfloat16)
    for dz in range(1, zc):
        rf_copy(dz).start()
    w_in.start()

    lax.fori_loop(0, nch + zc - 1 + LAG, tick, 0)

    def sent(j, width):
        for d in range(zc - 1):
            @pl.when((z + d < zc) & (z > 0))
            def _():
                left_copy(d, j, width).wait_send()

            @pl.when((z - d >= 0) & (z < zc - 1))
            def _():
                right_copy(d, j, width).wait_send()
        y_copy(j, width).wait_send()

    def drain(j, carry):
        either(j, sent)
        return carry

    lax.fori_loop(0, nch, drain, 0)
    for dz in range(1, zc):
        rf_copy(dz).wait_send()
        fwd_copy(dz, 0).wait_send()
        if share == 4:
            x_copy(dz).wait_send()
            fwd_copy(dz, 1).wait_send()


def body(weight, row_factors, col_factors, fitness_ranks):
    pop = lax.axis_size("pop")
    mb = fitness_ranks.shape[0]
    members = mb * pop
    zc = pop // 2
    rows, cols = weight.shape
    kb = -(-mb // 128) * 128
    nch = cols // WIDTH + 1
    share = 4 if rows % 32 == 0 and lax.axis_size("col") % 4 == 0 else 2
    anywhere = pl.BlockSpec(memory_space=pl.ANY)
    vmem = pl.BlockSpec(memory_space=pltpu.VMEM)
    dma = pltpu.SemaphoreType.DMA
    return pl.pallas_call(
        functools.partial(kernel, zc, members, share),
        out_shape=pltpu.VMEM((rows, cols), jnp.float32),
        in_specs=[vmem, vmem, anywhere, anywhere],
        out_specs=vmem,
        scratch_shapes=[
            pltpu.VMEM((mb, 128), jnp.float32),
            pltpu.VMEM((row_factors.shape[0], kb), jnp.bfloat16),
            pltpu.VMEM((mb, cols), jnp.bfloat16),
            pltpu.VMEM((nch, zc, kb, WIDTH), jnp.bfloat16),
            pltpu.VMEM((zc, 2 * rows, kb), jnp.bfloat16),
            pltpu.VMEM((nch, rows, WIDTH), jnp.bfloat16),
            pltpu.VMEM((nch, rows, WIDTH), jnp.bfloat16),
            pltpu.VMEM((rows, cols), jnp.float32),
            dma((2,)),
            dma((zc, nch)), dma((zc, nch)), dma((zc, nch)), dma((zc, nch)),
            dma((zc,)), dma((zc,)), dma((zc,)), dma((zc,)), dma((zc, 2)), dma((zc, 2)),
            dma((nch,)), dma((nch,)),
        ],
        compiler_params=pltpu.CompilerParams(
            collective_id=0, has_side_effects=True, vmem_limit_bytes=56 * 1024 * 1024),
        cost_estimate=pl.CostEstimate(
            flops=2 * rows * cols * members, bytes_accessed=8 * rows * cols, transcendentals=0),
    )(fitness_ranks.reshape(1, mb), row_factors.T, col_factors, weight)


def solution(mesh):
    in_specs = (P("pop", "col"), P(None, "pop"), P("pop", "col"), P("pop"))
    out_specs = P("pop", "col")
    return jax.shard_map(body, mesh=mesh, in_specs=in_specs, out_specs=out_specs, check_vma=False)
```
